256 devices in a mesh: grp: 4 (over z_hi, core), gx: 16 (over x, z_lo), gy: 4 (over y).
Axes of the slice: x: 4, y: 4, z: 8 (z_hi: 2, z_lo: 4; z = z_hi * 4 + z_lo), core: 2. Of those that a mesh axis runs over, the one named last changes fastest.
Arguments:
- wind_u: float32 [32, 1024, 1024], P('gx', 'grp', 'gy'), may hold values from -0.25 to 0.25
- wind_v: float32 [32, 1024, 1024], P('gx', 'grp', 'gy'), may hold values from -0.25 to 0.25
- theta: float32 [32, 1024, 1024], P('gx', 'grp', 'gy'), may hold values from 0.8 to 1.2
- ash: float32 [8, 32, 1024, 1024], P(None, None, ('grp', 'gx'), 'gy'), may hold values from 0.05 to 2
- src_x: int32 [16], replicated, may hold values from 0 to 1023
- src_y: int32 [16], replicated, may hold values from 0 to 1023
- src_rate: float32 [16, 8, 32], replicated, may hold values from 0.1 to 1
- settle_class: int32 [8], replicated, may hold values from 0 to 3
- settle_table: float32 [4], replicated, may hold values from 0.01 to 0.05
Outputs:
- ash_next: float32 [8, 32, 1024, 1024], P(None, None, ('grp', 'gx'), 'gy')
- met_next: float32 [3, 32, 1024, 1024], P(None, 'gx', 'grp', 'gy')
The draws below stay inside these ranges and needn't reach their ends.
All inputs are finite; a program needn't handle non-finite values.
Results may differ from the reference program's by a relative error of at most 0.00005.
Values sent between devices are 32-bit elements; how exact they have to be, the bound alone decides.
A program may use at most 128 MiB of HBM per device.

```python
import math
import jax
import jax.numpy as jnp
from jax import lax

B = 8
NCLS = 4
NSRC = 16
NX = 1024
NY = 1024
NZ = 32


def place_ends(values, key, low, top_value):
    longest = values.shape.index(max(values.shape))
    spots = []
    for shift in (0, 1):
        where = [jax.random.randint(jax.random.fold_in(key, axis), (), 0, length) for axis, length in enumerate(values.shape)]
        where[longest] = (where[longest] + shift) % values.shape[longest]
        spots.append(tuple(where))
    return values.at[spots[0]].set(low).at[spots[1]].set(top_value)


def shard_levels(rng, shape, shards, smallest, high):
    def one(position, shards_of):
        heights = jax.random.uniform(jax.random.fold_in(jax.random.fold_in(rng, 6), position), (shards_of,), jnp.float32, smallest / len(shards), high / len(shards))
        return jnp.repeat(jnp.exp(heights), shape[position] // shards_of).reshape((-1,) + (1,) * (len(shape) - position - 1))

    gain = one(*shards[0])
    for cut in shards[1:]:
        gain = gain * one(*cut)
    return gain


def setup_inputs(seed: int = 0) -> dict:
    key_list = jax.random.split(jax.random.key(seed), 10)
    return {
        "wind_u": jnp.clip(jax.random.uniform(key_list[0], (NZ, NX, NY), jnp.float32, -0.25, 0.25) * shard_levels(key_list[0], (NZ, NX, NY), ((0, 16), (1, 4), (2, 4)), -0.4, 0.0), -0.25, 0.25),
        "wind_v": jnp.clip(jax.random.uniform(key_list[1], (NZ, NX, NY), jnp.float32, -0.25, 0.25) * shard_levels(key_list[1], (NZ, NX, NY), ((0, 16), (1, 4), (2, 4)), -0.4, 0.0), -0.25, 0.25),
        "theta": jnp.clip(0.8 + 0.40000004 * jax.random.uniform(key_list[2], (NZ, NX, NY), jnp.float32) ** shard_levels(key_list[2], (NZ, NX, NY), ((0, 16), (1, 4), (2, 4)), -0.2, 0.2), 0.8, 1.2),
        "ash": jnp.clip(jnp.exp(math.log(2.0) - 3.6888794 * jax.random.uniform(key_list[3], (B, NZ, NX, NY), jnp.float32) ** shard_levels(key_list[3], (B, NZ, NX, NY), ((2, 64), (3, 4)), -0.2, 0.2)), 0.05, 2.0),
        "src_x": place_ends(jax.random.randint(key_list[4], (NSRC,), 0, NX), jax.random.fold_in(key_list[4], 1), 0, NX - 1).astype(jnp.int32),
        "src_y": place_ends(jax.random.randint(key_list[5], (NSRC,), 0, NY), jax.random.fold_in(key_list[5], 1), 0, NY - 1).astype(jnp.int32),
        "src_rate": jnp.clip(jnp.exp(jax.random.uniform(key_list[6], (NSRC, B, NZ), jnp.float32, math.log(0.1), math.log(1.0))), 0.1, 1.0),
        "settle_class": place_ends(jax.random.randint(key_list[7], (B,), 0, NCLS), jax.random.fold_in(key_list[7], 1), 0, NCLS - 1).astype(jnp.int32),
        "settle_table": jnp.clip(jnp.exp(jax.random.uniform(key_list[8], (NCLS,), jnp.float32, math.log(0.01), math.log(0.05))), 0.01, 0.05),
    }


diffuse_rate = 0.1
lift_scale = 0.1
lift_limit = 0.15
eddy_base = 0.005
eddy_slope = 0.03
mixing_base = 0.005
mixing_slope = 0.08
stable_weight = 20.0
level_decay = 32.0

def sides(field):
    padded = jnp.pad(field, ((0, 0), (1, 1), (1, 1)))
    return (padded[:, 2:, 1:-1], padded[:, :-2, 1:-1], padded[:, 1:-1, 2:], padded[:, 1:-1, :-2])

def vertical_sides(field):
    upper = jnp.concatenate([field[1:], field[-1:]], axis=0)
    lower = jnp.concatenate([field[:1], field[:-1]], axis=0)
    return (upper, lower)

def transport(conc, zonal, merid, lifted, eddy, mixing, settling):
    east, west, north, south = sides(conc)
    upper, lower = vertical_sides(conc)
    advect = jnp.maximum(zonal, 0.0) * (conc - west) + jnp.minimum(zonal, 0.0) * (east - conc)
    advect = advect + jnp.maximum(merid, 0.0) * (conc - south) + jnp.minimum(merid, 0.0) * (north - conc)
    advect = advect + jnp.maximum(lifted, 0.0) * (conc - lower) + jnp.minimum(lifted, 0.0) * (upper - conc)
    spread = eddy * (east + west + north + south - 4.0 * conc) + mixing * (upper - 2.0 * conc + lower)
    flux = settling * conc
    flux_above = jnp.concatenate([flux[1:], jnp.zeros_like(flux[:1])], axis=0)
    return conc - advect + spread + flux_above - flux

def reference(wind_u, wind_v, theta, ash, src_x, src_y, src_rate, settle_class, settle_table):
    zonal_east, zonal_west, zonal_north, zonal_south = sides(wind_u)
    merid_east, merid_west, merid_north, merid_south = sides(wind_v)
    warm_east, warm_west, warm_north, warm_south = sides(theta)
    xstretch = 0.5 * (zonal_east - zonal_west)
    yshear = 0.5 * (zonal_north - zonal_south)
    xshear = 0.5 * (merid_east - merid_west)
    ystretch = 0.5 * (merid_north - merid_south)
    divergence = xstretch + ystretch
    lifted = jnp.clip(-lift_scale * jnp.cumsum(divergence, axis=0), -lift_limit, lift_limit)
    zonal_up, zonal_down = vertical_sides(wind_u)
    merid_up, merid_down = vertical_sides(wind_v)
    warm_up, warm_down = vertical_sides(theta)
    zonal_slope = 0.5 * (zonal_up - zonal_down)
    merid_slope = 0.5 * (merid_up - merid_down)
    warm_slope = 0.5 * (warm_up - warm_down)
    zonal_lap = zonal_east + zonal_west + zonal_north + zonal_south - 4.0 * wind_u
    merid_lap = merid_east + merid_west + merid_north + merid_south - 4.0 * wind_v
    met_next = jnp.stack([wind_u + diffuse_rate * zonal_lap - lifted * zonal_slope, wind_v + diffuse_rate * merid_lap - lifted * merid_slope, theta - lifted * warm_slope])
    eddy = eddy_base + eddy_slope * jnp.sqrt((xstretch - ystretch) ** 2 + (yshear + xshear) ** 2)
    mixing = mixing_base + mixing_slope * jnp.sqrt(zonal_slope ** 2 + merid_slope ** 2) / (1.0 + stable_weight * jnp.maximum(warm_slope, 0.0))
    level = jnp.arange(NZ, dtype=jnp.float32)
    density = jnp.sqrt(theta) * jnp.exp(level / level_decay)[:, None, None]
    speeds = settle_table[settle_class]

    def one_bin(item):
        field, speed, rate = item
        conc = field.at[:, src_x, src_y].add(rate.T)
        return transport(conc, wind_u, wind_v, lifted, eddy, mixing, speed * density)
    ash_next = lax.map(one_bin, (ash, speeds, jnp.transpose(src_rate, (1, 0, 2))))
    return (ash_next, met_next)
```

```python
import functools

import jax
import jax.numpy as jnp
from jax import lax
from jax.experimental import pallas as pl
from jax.experimental.pallas import tpu as pltpu
from jax.sharding import PartitionSpec as P

MESH = pl.DeviceIdType.MESH
F32 = jnp.float32

diffuse_rate = 0.1
lift_scale = 0.1
lift_limit = 0.15
eddy_base = 0.005
eddy_slope = 0.03
mixing_base = 0.005
mixing_slope = 0.08
stable_weight = 20.0
level_decay = 32.0

G = 16
GRP = 4
GY = 4
LV = 2
NZ = 32
ROWS = 16
COLS = 256
MROWS = 256
BINS = 8
NSRC = 16


def kernel(
    u_ref, v_ref, t_ref, ash_ref, sx_ref, sy_ref, rate_ref, class_ref, table_ref,
    ash_out, met_out,
    uv, fields, conc, result, ret, coef, dens, marks,
    row_send, row_recv, col_send, col_recv, edge_send, edge_recv,
    arow_send, arow_recv, acol_send, acol_recv,
    bulk_s, bulk_r, edge_s, edge_r, ret_s, ret_r, near_s, near_r, local,
):
    grp, gx, gy = lax.axis_index("grp"), lax.axis_index("gx"), lax.axis_index("gy")
    line = grp * G + gx
    last_line = GRP * G - 1
    wrap_up, wrap_down = gx == G - 1, gx == 0
    row_up = (grp + wrap_up.astype(jnp.int32), lax.rem(gx + 1, G), gy)
    row_down = (grp - wrap_down.astype(jnp.int32), lax.rem(gx + G - 1, G), gy)

    met_in = [
        pltpu.make_async_copy(u_ref, uv.at[0], local.at[0]),
        pltpu.make_async_copy(v_ref, uv.at[1], local.at[1]),
    ]
    ash_in = pltpu.make_async_copy(ash_ref, conc, local.at[2])
    for copy in met_in:
        copy.start()
    ash_in.start()

    barrier = pltpu.get_barrier_semaphore()

    def greet(device):
        pl.semaphore_signal(barrier, inc=1, device_id=device, device_id_type=MESH)

    for d in range(1, G):
        greet((grp, jnp.bitwise_xor(gx, d), gy))
    pl.when(gy > 0)(lambda: greet((grp, gx, gy - 1)))
    pl.when(gy < GY - 1)(lambda: greet((grp, gx, gy + 1)))
    pl.when(grp > 0)(lambda: greet((grp - 1, gx, gy)))
    pl.when(grp < GRP - 1)(lambda: greet((grp + 1, gx, gy)))
    far_down = jnp.logical_and(wrap_down, grp > 0)
    far_up = jnp.logical_and(wrap_up, grp < GRP - 1)
    pl.when(far_down)(lambda: greet(row_down))
    pl.when(far_up)(lambda: greet(row_up))
    count = (
        G - 1
        + (gy > 0).astype(jnp.int32) + (gy < GY - 1).astype(jnp.int32)
        + (grp > 0).astype(jnp.int32) + (grp < GRP - 1).astype(jnp.int32)
        + far_down.astype(jnp.int32) + far_up.astype(jnp.int32)
    )
    pl.semaphore_wait(barrier, count)

    def remote(src, dst, send, recv, device):
        return pltpu.make_async_remote_copy(
            src_ref=src, dst_ref=dst, send_sem=send, recv_sem=recv,
            device_id=device, device_id_type=MESH,
        )

    sources = (u_ref, v_ref, t_ref)
    own_levels = pl.ds(LV * gx, LV)
    own_rows = pl.ds(pl.multiple_of(gx * ROWS, ROWS), ROWS)
    bulk = []
    for d in range(1, G):
        peer = jnp.bitwise_xor(gx, d)
        rows = pl.ds(pl.multiple_of(peer * ROWS, ROWS), ROWS)
        for f in range(3):
            copy = remote(
                sources[f].at[:, rows, :], fields.at[f, own_levels],
                bulk_s.at[f, d], bulk_r.at[f, d], (grp, peer, gy),
            )
            copy.start()
            bulk.append(copy)
    own_bulk = []
    for f in range(3):
        copy = pltpu.make_async_copy(
            sources[f].at[:, own_rows, :], fields.at[f, own_levels], local.at[3 + f]
        )
        copy.start()
        own_bulk.append(copy)

    lane = lax.broadcasted_iota(jnp.int32, (8, 128), 1)
    for copy in met_in:
        copy.wait()
    for f in range(2):
        for lev in range(LV):
            at = 2 * f + lev
            row_send[0, at : at + 1, :] = uv[f, lev, MROWS - 8 : MROWS, :][7:8]
            row_send[1, at : at + 1, :] = uv[f, lev, 0:8, :][0:1]
    row_send[0, 4:8, :] = jnp.zeros((4, COLS), F32)
    row_send[1, 4:8, :] = jnp.zeros((4, COLS), F32)

    def pack_columns(g, _):
        start = pl.multiple_of(g * ROWS, ROWS)
        right = jnp.zeros((8, 128), F32)
        left = jnp.zeros((8, 128), F32)
        for half in range(2):
            rows = pl.ds(start + 8 * half, 8)
            for f in range(2):
                for lev in range(LV):
                    c = 64 * half + 2 * f + lev
                    tail = uv[f, lev, rows, 128:256]
                    right = jnp.where(lane == c, pltpu.roll(tail, c + 1, 1), right)
                    head = uv[f, lev, rows, 0:128]
                    left = jnp.where(lane == c + 4, pltpu.roll(head, c + 4, 1), left)
        col_send[0, g] = right
        col_send[1, g] = left
        return 0

    lax.fori_loop(0, G, pack_columns, 0)

    rows_up = remote(row_send.at[0], row_recv.at[0], near_s.at[0], near_r.at[0], (grp + 1, gx, gy))
    rows_down = remote(row_send.at[1], row_recv.at[1], near_s.at[1], near_r.at[1], (grp - 1, gx, gy))
    cols_up = remote(col_send.at[0], col_recv.at[0], near_s.at[2], near_r.at[2], (grp, gx, gy + 1))
    cols_down = remote(col_send.at[1], col_recv.at[1], near_s.at[3], near_r.at[3], (grp, gx, gy - 1))

    def clear(ref):
        ref[...] = jnp.zeros(ref.shape, F32)

    pl.when(gy < GY - 1)(cols_up.start)
    pl.when(gy > 0)(cols_down.start)
    pl.when(grp < GRP - 1)(rows_up.start)
    pl.when(grp > 0)(rows_down.start)
    pl.when(grp == 0)(lambda: clear(row_recv.at[0]))
    pl.when(grp == GRP - 1)(lambda: clear(row_recv.at[1]))
    pl.when(gy == 0)(lambda: clear(col_recv.at[0]))
    pl.when(gy == GY - 1)(lambda: clear(col_recv.at[1]))

    def pack_rows(g, _):
        before = pl.ds(pl.multiple_of(jnp.maximum(g * ROWS - 8, 0), 8), 8)
        after = pl.ds(pl.multiple_of(jnp.minimum(g * ROWS + ROWS, MROWS - 8), 8), 8)
        for f in range(2):
            for lev in range(LV):
                at = 2 * f + lev
                edge_send[g, at : at + 1, 0:COLS] = uv[f, lev, before, :][7:8]
                edge_send[g, at + 4 : at + 5, 0:COLS] = uv[f, lev, after, :][0:1]
        return 0

    lax.fori_loop(0, G, pack_rows, 0)
    pl.when(grp > 0)(rows_up.wait_recv)
    pl.when(grp < GRP - 1)(rows_down.wait_recv)
    pl.when(gy > 0)(cols_up.wait_recv)
    pl.when(gy < GY - 1)(cols_down.wait_recv)
    edge_send[0, 0:4, 0:COLS] = row_recv[0, 0:4, :]
    edge_send[G - 1, 4:8, 0:COLS] = row_recv[1, 0:4, :]

    def merge_columns(g, _):
        edge_send[g, :, COLS : COLS + 128] = jnp.where(
            lane % 64 < 4, col_recv[0, g], col_recv[1, g]
        )
        return 0

    lax.fori_loop(0, G, merge_columns, 0)
    edges = []
    for d in range(1, G):
        peer = jnp.bitwise_xor(gx, d)
        copy = remote(
            edge_send.at[peer], edge_recv.at[gx], edge_s.at[d], edge_r.at[d], (grp, peer, gy)
        )
        copy.start()
        edges.append(copy)
    own_edge = pltpu.make_async_copy(edge_send.at[gx], edge_recv.at[gx], local.at[6])
    own_edge.start()

    row16 = lax.broadcasted_iota(jnp.int32, (ROWS, COLS), 0)
    lane16 = lax.broadcasted_iota(jnp.int32, (ROWS, COLS), 1)
    start_x, start_y = line * ROWS, gy * COLS

    def mark(s, _):
        hit = jnp.logical_and(row16 == sx_ref[s] - start_x, lane16 == sy_ref[s] - start_y)
        marks[s] = jnp.where(hit, 1.0, 0.0).astype(F32)
        return 0

    lax.fori_loop(0, NSRC, mark, 0)
    ash_in.wait()

    def emit(k, _):
        for b in range(BINS):
            total = conc[b, k]
            for s in range(NSRC):
                total = total + marks[s] * rate_ref[s, b, k]
            conc[b, k] = total
        return 0

    lax.fori_loop(0, NZ, emit, 0)

    lane128 = lax.broadcasted_iota(jnp.int32, (ROWS, 128), 1)

    def pack_ash(k, sums):
        sums = list(sums)
        for b in range(BINS):
            slab = conc[b, k]
            arow_send[0, b, pl.ds(k, 1), :] = slab[ROWS - 1 : ROWS]
            arow_send[1, b, pl.ds(k, 1), :] = slab[0:1]
            at = (b % 4) * NZ + k
            spot = lane128 == at
            right = pltpu.roll(slab[:, 128:256], lax.rem(at + 1, 128), 1)
            left = pltpu.roll(slab[:, 0:128], at, 1)
            sums[b // 4] = jnp.where(spot, right, sums[b // 4])
            sums[2 + b // 4] = jnp.where(spot, left, sums[2 + b // 4])
        return tuple(sums)

    packed = lax.fori_loop(0, NZ, pack_ash, tuple(jnp.zeros((ROWS, 128), F32) for _ in range(4)))
    for side in range(2):
        for part in range(2):
            acol_send[side, part] = packed[2 * side + part]

    arows_up = remote(arow_send.at[0], arow_recv.at[0], near_s.at[4], near_r.at[4], row_up)
    arows_down = remote(arow_send.at[1], arow_recv.at[1], near_s.at[5], near_r.at[5], row_down)
    acols_up = remote(acol_send.at[0], acol_recv.at[0], near_s.at[6], near_r.at[6], (grp, gx, gy + 1))
    acols_down = remote(acol_send.at[1], acol_recv.at[1], near_s.at[7], near_r.at[7], (grp, gx, gy - 1))
    pl.when(line < last_line)(arows_up.start)
    pl.when(line > 0)(arows_down.start)
    pl.when(gy < GY - 1)(acols_up.start)
    pl.when(gy > 0)(acols_down.start)
    pl.when(line == 0)(lambda: clear(arow_recv.at[0]))
    pl.when(line == last_line)(lambda: clear(arow_recv.at[1]))
    pl.when(gy == 0)(lambda: clear(acol_recv.at[0]))
    pl.when(gy == GY - 1)(lambda: clear(acol_recv.at[1]))

    for copy in bulk:
        copy.wait_recv()
    for copy in edges:
        copy.wait_recv()
    for copy in own_bulk:
        copy.wait()
    own_edge.wait()

    first_row, end_row = row16 == 0, row16 == ROWS - 1
    first_lane, end_lane = lane16 == 0, lane16 == COLS - 1

    def twice(half):
        return jnp.concatenate([half, half], axis=1)

    def along_x(field, below, above):
        east = jnp.where(end_row, above, pltpu.roll(field, ROWS - 1, 0))
        west = jnp.where(first_row, below, pltpu.roll(field, 1, 0))
        return east, west

    def along_y(field, below, above):
        north = jnp.where(end_lane, twice(above), pltpu.roll(field, COLS - 1, 1))
        south = jnp.where(first_lane, twice(below), pltpu.roll(field, 1, 1))
        return north, south

    def diagnose(g, total):
        edge_cols = edge_recv[g, :, COLS : COLS + 128]
        for lev in range(LV):
            k = LV * g + lev
            up, down = jnp.minimum(k + 1, NZ - 1), jnp.maximum(k - 1, 0)
            wind = []
            for f in range(2):
                at = 2 * f + lev
                field = fields[f, k]
                east, west = along_x(
                    field,
                    edge_recv[g, at : at + 1, 0:COLS],
                    edge_recv[g, at + 4 : at + 5, 0:COLS],
                )
                below = jnp.concatenate(
                    [pltpu.roll(edge_cols, (128 - at) % 128, 1), pltpu.roll(edge_cols, 64 - at, 1)], axis=0
                )
                above = jnp.concatenate(
                    [pltpu.roll(edge_cols, 127 - at - 4, 1), pltpu.roll(edge_cols, 63 - at - 4, 1)], axis=0
                )
                north, south = along_y(field, below, above)
                slope = 0.5 * (fields[f, up] - fields[f, down])
                wind.append((field, east, west, north, south, slope))
            warm = fields[2, k]
            warm_slope = 0.5 * (fields[2, up] - fields[2, down])
            (u, ue, uw, un, us, u_slope), (v, ve, vw, vn, vs, v_slope) = wind
            xstretch, yshear = 0.5 * (ue - uw), 0.5 * (un - us)
            xshear, ystretch = 0.5 * (ve - vw), 0.5 * (vn - vs)
            total = total + (xstretch + ystretch)
            lift = jnp.clip(-lift_scale * total, -lift_limit, lift_limit)
            ret[0, k] = u + diffuse_rate * (ue + uw + un + us - 4.0 * u) - lift * u_slope
            ret[1, k] = v + diffuse_rate * (ve + vw + vn + vs - 4.0 * v) - lift * v_slope
            ret[2, k] = warm - lift * warm_slope
            eddy = eddy_base + eddy_slope * jnp.sqrt((xstretch - ystretch) ** 2 + (yshear + xshear) ** 2)
            mixing = mixing_base + mixing_slope * jnp.sqrt(u_slope**2 + v_slope**2) / (
                1.0 + stable_weight * jnp.maximum(warm_slope, 0.0)
            )
            height = jnp.exp(jnp.zeros((1, COLS), F32) + k.astype(F32) * (1.0 / level_decay))
            dens[k] = jnp.sqrt(warm) * height
            coef[0, k] = eddy - jnp.minimum(u, 0.0)
            coef[1, k] = eddy + jnp.maximum(u, 0.0)
            coef[2, k] = eddy - jnp.minimum(v, 0.0)
            coef[3, k] = eddy + jnp.maximum(v, 0.0)
            coef[4, k] = mixing - jnp.minimum(lift, 0.0)
            coef[5, k] = mixing + jnp.maximum(lift, 0.0)
            coef[6, k] = 1.0 - (jnp.abs(u) + jnp.abs(v) + jnp.abs(lift) + 4.0 * eddy + 2.0 * mixing)
        return total

    lax.fori_loop(0, G, diagnose, jnp.zeros((ROWS, COLS), F32))
    dens[NZ] = jnp.zeros((ROWS, COLS), F32)

    returns = []
    for d in range(1, G):
        peer = jnp.bitwise_xor(gx, d)
        copy = remote(
            ret.at[:, pl.ds(LV * peer, LV)], met_out.at[:, :, own_rows, :],
            ret_s.at[d], ret_r.at[d], (grp, peer, gy),
        )
        copy.start()
        returns.append(copy)
    own_return = pltpu.make_async_copy(
        ret.at[:, own_levels], met_out.at[:, :, own_rows, :], local.at[7]
    )
    own_return.start()

    pl.when(line > 0)(arows_up.wait_recv)
    pl.when(line < last_line)(arows_down.wait_recv)
    pl.when(gy > 0)(acols_up.wait_recv)
    pl.when(gy < GY - 1)(acols_down.wait_recv)

    for b in range(BINS):
        speed = table_ref[class_ref[b]]

        def transport(k, _, b=b, speed=speed):
            here = conc[b, k]
            upper, lower = conc[b, jnp.minimum(k + 1, NZ - 1)], conc[b, jnp.maximum(k - 1, 0)]
            at = (b % 4) * NZ + k
            east, west = along_x(
                here, arow_recv[0, b, pl.ds(k, 1), :], arow_recv[1, b, pl.ds(k, 1), :]
            )
            below = pltpu.roll(acol_recv[0, b // 4], lax.rem(128 - at, 128), 1)
            above = pltpu.roll(acol_recv[1, b // 4], 127 - at, 1)
            north, south = along_y(here, below, above)
            out = here * (coef[6, k] - speed * dens[k]) + upper * (coef[4, k] + speed * dens[k + 1])
            out = out + east * coef[0, k] + west * coef[1, k]
            out = out + north * coef[2, k] + south * coef[3, k]
            result[b, k] = out + lower * coef[5, k]
            return 0

        lax.fori_loop(0, NZ, transport, 0)
        pltpu.make_async_copy(result.at[b], ash_out.at[b], local.at[8 + b]).start()

    for copy in returns:
        copy.wait_recv()
    own_return.wait()
    for b in range(BINS):
        pltpu.make_async_copy(result.at[b], ash_out.at[b], local.at[8 + b]).wait()
    for copy in bulk + edges + returns:
        copy.wait_send()
    pl.when(grp < GRP - 1)(rows_up.wait_send)
    pl.when(grp > 0)(rows_down.wait_send)
    pl.when(gy < GY - 1)(cols_up.wait_send)
    pl.when(gy > 0)(cols_down.wait_send)
    pl.when(line < last_line)(arows_up.wait_send)
    pl.when(line > 0)(arows_down.wait_send)
    pl.when(gy < GY - 1)(acols_up.wait_send)
    pl.when(gy > 0)(acols_down.wait_send)


def body(wind_u, wind_v, theta, ash, src_x, src_y, src_rate, settle_class, settle_table):
    hbm = pl.BlockSpec(memory_space=pl.ANY)
    smem = pl.BlockSpec(memory_space=pltpu.SMEM)
    dma = pltpu.SemaphoreType.DMA
    return tuple(
        pl.pallas_call(
            kernel,
            out_shape=(
                jax.ShapeDtypeStruct((BINS, NZ, ROWS, COLS), F32),
                jax.ShapeDtypeStruct((3, LV, MROWS, COLS), F32),
            ),
            in_specs=[hbm] * 4 + [smem] * 5,
            out_specs=(hbm, hbm),
            scratch_shapes=[
                pltpu.VMEM((2, LV, MROWS, COLS), F32),
                pltpu.VMEM((3, NZ, ROWS, COLS), F32),
                pltpu.VMEM((BINS, NZ, ROWS, COLS), F32),
                pltpu.VMEM((BINS, NZ, ROWS, COLS), F32),
                pltpu.VMEM((3, NZ, ROWS, COLS), F32),
                pltpu.VMEM((7, NZ, ROWS, COLS), F32),
                pltpu.VMEM((NZ + 1, ROWS, COLS), F32),
                pltpu.VMEM((NSRC, ROWS, COLS), F32),
                pltpu.VMEM((2, 8, COLS), F32),
                pltpu.VMEM((2, 8, COLS), F32),
                pltpu.VMEM((2, G, 8, 128), F32),
                pltpu.VMEM((2, G, 8, 128), F32),
                pltpu.VMEM((G, 8, COLS + 128), F32),
                pltpu.VMEM((G, 8, COLS + 128), F32),
                pltpu.VMEM((2, BINS, NZ, COLS), F32),
                pltpu.VMEM((2, BINS, NZ, COLS), F32),
                pltpu.VMEM((2, 2, ROWS, 128), F32),
                pltpu.VMEM((2, 2, ROWS, 128), F32),
                dma((3, G)), dma((3, G)),
                dma((G,)), dma((G,)),
                dma((G,)), dma((G,)),
                dma((8,)), dma((8,)),
                dma((16,)),
            ],
            compiler_params=pltpu.CompilerParams(
                collective_id=0, has_side_effects=True, vmem_limit_bytes=40 * 2**20
            ),
        )(wind_u, wind_v, theta, ash, src_x, src_y, src_rate, settle_class, settle_table)
    )


def solution(mesh):
    in_specs = (
        P("gx", "grp", "gy"),
        P("gx", "grp", "gy"),
        P("gx", "grp", "gy"),
        P(None, None, ("grp", "gx"), "gy"),
        P(),
        P(),
        P(),
        P(),
        P(),
    )
    out_specs = (P(None, None, ("grp", "gx"), "gy"), P(None, "gx", "grp", "gy"))
    return jax.shard_map(body, mesh=mesh, in_specs=in_specs, out_specs=out_specs, check_vma=False)
```

```python
import functools

import jax
import jax.numpy as jnp
from jax import lax
from jax.experimental import pallas as pl
from jax.experimental.pallas import tpu as pltpu
from jax.sharding import PartitionSpec as P

MESH = pl.DeviceIdType.MESH
F32 = jnp.float32

diffuse_rate = 0.1
lift_scale = 0.1
lift_limit = 0.15
eddy_base = 0.005
eddy_slope = 0.03
mixing_base = 0.005
mixing_slope = 0.08
stable_weight = 20.0
level_decay = 32.0

G = 16
GRP = 4
GY = 4
LV = 2
NZ = 32
ROWS = 16
COLS = 256
MROWS = 256
BINS = 8
NSRC = 16


def kernel(
    u_ref, v_ref, t_ref, ash_ref, sx_hbm, sy_hbm, rate_hbm, class_hbm, table_hbm,
    ash_out, met_out,
    sx_ref, sy_ref, rate_ref, class_ref, table_ref,
    met, partner, lift_recv, fields, conc, ret, lifts, coef, dens, marks,
    row_send, row_recv, col_send, col_recv, edge_send, edge_recv,
    arow_send, arow_recv, acol_send, acol_recv,
    bulk_s, bulk_r, edge_s, edge_r, ret_s, ret_r, lift_s, lift_r, part_s, part_r, near_s, near_r, local,
):
    grp, gx, gy = lax.axis_index("grp"), lax.axis_index("gx"), lax.axis_index("gy")
    line = grp * G + gx
    last_line = GRP * G - 1
    wrap_up, wrap_down = gx == G - 1, gx == 0
    row_up = (grp + wrap_up.astype(jnp.int32), lax.rem(gx + 1, G), gy)
    row_down = (grp - wrap_down.astype(jnp.int32), lax.rem(gx + G - 1, G), gy)

    sources = (u_ref, v_ref, t_ref)
    met_in = [pltpu.make_async_copy(sources[f], met.at[f], local.at[f]) for f in range(3)]
    ash_in = pltpu.make_async_copy(ash_ref, conc, local.at[3])
    small_in = [
        pltpu.make_async_copy(src, dst, local.at[8 + i])
        for i, (src, dst) in enumerate(
            (
                (sx_hbm, sx_ref), (sy_hbm, sy_ref), (rate_hbm, rate_ref),
                (class_hbm, class_ref), (table_hbm, table_ref),
            )
        )
    ]
    for copy in met_in + [ash_in] + small_in:
        copy.start()

    barrier = pltpu.get_barrier_semaphore()

    def greet(device):
        pl.semaphore_signal(barrier, inc=1, device_id=device, device_id_type=MESH)

    for d in range(1, G):
        greet((grp, jnp.bitwise_xor(gx, d), gy))
    pl.when(gy > 0)(lambda: greet((grp, gx, gy - 1)))
    pl.when(gy < GY - 1)(lambda: greet((grp, gx, gy + 1)))
    pl.when(grp > 0)(lambda: greet((grp - 1, gx, gy)))
    pl.when(grp < GRP - 1)(lambda: greet((grp + 1, gx, gy)))
    far_down = jnp.logical_and(wrap_down, grp > 0)
    far_up = jnp.logical_and(wrap_up, grp < GRP - 1)
    pl.when(far_down)(lambda: greet(row_down))
    pl.when(far_up)(lambda: greet(row_up))
    count = (
        G - 1
        + (gy > 0).astype(jnp.int32) + (gy < GY - 1).astype(jnp.int32)
        + (grp > 0).astype(jnp.int32) + (grp < GRP - 1).astype(jnp.int32)
        + far_down.astype(jnp.int32) + far_up.astype(jnp.int32)
    )
    pl.semaphore_wait(barrier, count)

    def remote(src, dst, send, recv, device):
        return pltpu.make_async_remote_copy(
            src_ref=src, dst_ref=dst, send_sem=send, recv_sem=recv,
            device_id=device, device_id_type=MESH,
        )

    own_levels = pl.ds(LV * gx, LV)
    own_x, own_z = gx // 4, gx % 4
    bulk = []
    for d in range(1, G):
        peer = jnp.bitwise_xor(gx, d)
        for f in range(3):
            copy = remote(
                sources[f].at[:, peer // 4, peer % 4], fields.at[f, own_levels],
                bulk_s.at[f, d], bulk_r.at[f, d], (grp, peer, gy),
            )
            copy.start()
            bulk.append(copy)
    own_bulk = []
    for f in range(3):
        copy = pltpu.make_async_copy(
            sources[f].at[:, own_x, own_z], fields.at[f, own_levels], local.at[4 + f]
        )
        copy.start()
        own_bulk.append(copy)

    mine = 1 - gx % 2
    mate = jnp.bitwise_xor(gx, 1)
    pairs = []
    for j in range(1, 4):
        group = jnp.bitwise_xor(mate % 4, j)
        for f in range(3):
            copy = remote(
                sources[f].at[mine, :, group], partner.at[f, :, group],
                part_s.at[f, j], part_r.at[f, j], (grp, mate, gy),
            )
            copy.start()
            pairs.append(copy)

    lane = lax.broadcasted_iota(jnp.int32, (8, 128), 1)
    for copy in met_in:
        copy.wait()
    for f in range(2):
        for lev in range(LV):
            at = 2 * f + lev
            row_send[0, at : at + 1, :] = met[f, lev, 3, 3, ROWS - 1 : ROWS, :]
            row_send[1, at : at + 1, :] = met[f, lev, 0, 0, 0:1, :]
    row_send[0, 4:8, :] = jnp.zeros((4, COLS), F32)
    row_send[1, 4:8, :] = jnp.zeros((4, COLS), F32)

    def pack_columns(g, _):
        right = jnp.zeros((8, 128), F32)
        left = jnp.zeros((8, 128), F32)
        for half in range(2):
            rows = slice(8 * half, 8 * half + 8)
            for f in range(2):
                for lev in range(LV):
                    c = 64 * half + 2 * f + lev
                    tail = met[f, lev, g // 4, g % 4, rows, 128:256]
                    right = jnp.where(lane == c, pltpu.roll(tail, c + 1, 1), right)
                    head = met[f, lev, g // 4, g % 4, rows, 0:128]
                    left = jnp.where(lane == c + 4, pltpu.roll(head, c + 4, 1), left)
        col_send[0, g] = right
        col_send[1, g] = left
        return 0

    lax.fori_loop(0, G, pack_columns, 0)

    rows_up = remote(row_send.at[0], row_recv.at[0], near_s.at[0], near_r.at[0], (grp + 1, gx, gy))
    rows_down = remote(row_send.at[1], row_recv.at[1], near_s.at[1], near_r.at[1], (grp - 1, gx, gy))
    cols_up = remote(col_send.at[0], col_recv.at[0], near_s.at[2], near_r.at[2], (grp, gx, gy + 1))
    cols_down = remote(col_send.at[1], col_recv.at[1], near_s.at[3], near_r.at[3], (grp, gx, gy - 1))

    def clear(ref):
        ref[...] = jnp.zeros(ref.shape, F32)

    pl.when(gy < GY - 1)(cols_up.start)
    pl.when(gy > 0)(cols_down.start)
    pl.when(grp < GRP - 1)(rows_up.start)
    pl.when(grp > 0)(rows_down.start)
    pl.when(grp == 0)(lambda: clear(row_recv.at[0]))
    pl.when(grp == GRP - 1)(lambda: clear(row_recv.at[1]))
    pl.when(gy == 0)(lambda: clear(col_recv.at[0]))
    pl.when(gy == GY - 1)(lambda: clear(col_recv.at[1]))

    def pack_rows(g, _):
        before, after = jnp.maximum(g - 1, 0), jnp.minimum(g + 1, G - 1)
        for f in range(2):
            for lev in range(LV):
                at = 2 * f + lev
                edge_send[g, at : at + 1, 0:COLS] = met[f, lev, before // 4, before % 4, ROWS - 1 : ROWS, :]
                edge_send[g, at + 4 : at + 5, 0:COLS] = met[f, lev, after // 4, after % 4, 0:1, :]
        return 0

    lax.fori_loop(0, G, pack_rows, 0)
    pl.when(grp > 0)(rows_up.wait_recv)
    pl.when(grp < GRP - 1)(rows_down.wait_recv)
    pl.when(gy > 0)(cols_up.wait_recv)
    pl.when(gy < GY - 1)(cols_down.wait_recv)
    edge_send[0, 0:4, 0:COLS] = row_recv[0, 0:4, :]
    edge_send[G - 1, 4:8, 0:COLS] = row_recv[1, 0:4, :]

    def merge_columns(g, _):
        edge_send[g, :, COLS : COLS + 128] = jnp.where(
            lane % 64 < 4, col_recv[0, g], col_recv[1, g]
        )
        return 0

    lax.fori_loop(0, G, merge_columns, 0)
    edges = []
    for d in range(1, G):
        peer = jnp.bitwise_xor(gx, d)
        copy = remote(
            edge_send.at[peer], edge_recv.at[gx], edge_s.at[d], edge_r.at[d], (grp, peer, gy)
        )
        copy.start()
        edges.append(copy)
    own_edge = pltpu.make_async_copy(edge_send.at[gx], edge_recv.at[gx], local.at[7])
    own_edge.start()

    row16 = lax.broadcasted_iota(jnp.int32, (ROWS, COLS), 0)
    lane16 = lax.broadcasted_iota(jnp.int32, (ROWS, COLS), 1)
    start_x, start_y = line * ROWS, gy * COLS

    for copy in small_in:
        copy.wait()

    def mark(s, _):
        hit = jnp.logical_and(row16 == sx_ref[s] - start_x, lane16 == sy_ref[s] - start_y)
        marks[s] = jnp.where(hit, 1.0, 0.0).astype(F32)
        return 0

    lax.fori_loop(0, NSRC, mark, 0)
    ash_in.wait()

    def emit(k, _):
        for b in range(BINS):
            total = conc[b, k]
            for s in range(NSRC):
                total = total + marks[s] * rate_ref[s, b, k]
            conc[b, k] = total
        return 0

    lax.fori_loop(0, NZ, emit, 0)

    lane128 = lax.broadcasted_iota(jnp.int32, (ROWS, 128), 1)

    def pack_ash(k, sums):
        sums = list(sums)
        for b in range(BINS):
            slab = conc[b, k]
            arow_send[0, b, pl.ds(k, 1), :] = slab[ROWS - 1 : ROWS]
            arow_send[1, b, pl.ds(k, 1), :] = slab[0:1]
            at = (b % 4) * NZ + k
            spot = lane128 == at
            right = pltpu.roll(slab[:, 128:256], lax.rem(at + 1, 128), 1)
            left = pltpu.roll(slab[:, 0:128], at, 1)
            sums[b // 4] = jnp.where(spot, right, sums[b // 4])
            sums[2 + b // 4] = jnp.where(spot, left, sums[2 + b // 4])
        return tuple(sums)

    packed = lax.fori_loop(0, NZ, pack_ash, tuple(jnp.zeros((ROWS, 128), F32) for _ in range(4)))
    for side in range(2):
        for part in range(2):
            acol_send[side, part] = packed[2 * side + part]

    arows_up = remote(arow_send.at[0], arow_recv.at[0], near_s.at[4], near_r.at[4], row_up)
    arows_down = remote(arow_send.at[1], arow_recv.at[1], near_s.at[5], near_r.at[5], row_down)
    acols_up = remote(acol_send.at[0], acol_recv.at[0], near_s.at[6], near_r.at[6], (grp, gx, gy + 1))
    acols_down = remote(acol_send.at[1], acol_recv.at[1], near_s.at[7], near_r.at[7], (grp, gx, gy - 1))
    pl.when(line < last_line)(arows_up.start)
    pl.when(line > 0)(arows_down.start)
    pl.when(gy < GY - 1)(acols_up.start)
    pl.when(gy > 0)(acols_down.start)
    pl.when(line == 0)(lambda: clear(arow_recv.at[0]))
    pl.when(line == last_line)(lambda: clear(arow_recv.at[1]))
    pl.when(gy == 0)(lambda: clear(acol_recv.at[0]))
    pl.when(gy == GY - 1)(lambda: clear(acol_recv.at[1]))

    for copy in bulk:
        copy.wait_recv()
    for copy in edges:
        copy.wait_recv()
    for copy in own_bulk:
        copy.wait()
    own_edge.wait()

    first_row, end_row = row16 == 0, row16 == ROWS - 1
    first_lane, end_lane = lane16 == 0, lane16 == COLS - 1

    def twice(half):
        return jnp.concatenate([half, half], axis=1)

    def along_x(field, below, above):
        east = jnp.where(end_row, above, pltpu.roll(field, ROWS - 1, 0))
        west = jnp.where(first_row, below, pltpu.roll(field, 1, 0))
        return east, west

    def along_y(field, below, above):
        north = jnp.where(end_lane, twice(above), pltpu.roll(field, COLS - 1, 1))
        south = jnp.where(first_lane, twice(below), pltpu.roll(field, 1, 1))
        return north, south

    def diagnose(g, total):
        edge_cols = edge_recv[g, :, COLS : COLS + 128]
        for lev in range(LV):
            k = LV * g + lev
            up, down = jnp.minimum(k + 1, NZ - 1), jnp.maximum(k - 1, 0)
            wind = []
            for f in range(2):
                at = 2 * f + lev
                field = fields[f, k]
                east, west = along_x(
                    field,
                    edge_recv[g, at : at + 1, 0:COLS],
                    edge_recv[g, at + 4 : at + 5, 0:COLS],
                )
                below = jnp.concatenate(
                    [pltpu.roll(edge_cols, (128 - at) % 128, 1), pltpu.roll(edge_cols, 64 - at, 1)], axis=0
                )
                above = jnp.concatenate(
                    [pltpu.roll(edge_cols, 127 - at - 4, 1), pltpu.roll(edge_cols, 63 - at - 4, 1)], axis=0
                )
                north, south = along_y(field, below, above)
                slope = 0.5 * (fields[f, up] - fields[f, down])
                wind.append((field, east, west, north, south, slope))
            warm = fields[2, k]
            warm_slope = 0.5 * (fields[2, up] - fields[2, down])
            (u, ue, uw, un, us, u_slope), (v, ve, vw, vn, vs, v_slope) = wind
            xstretch, yshear = 0.5 * (ue - uw), 0.5 * (un - us)
            xshear, ystretch = 0.5 * (ve - vw), 0.5 * (vn - vs)
            total = total + (xstretch + ystretch)
            lift = jnp.clip(-lift_scale * total, -lift_limit, lift_limit)
            ret[0, k] = u + diffuse_rate * (ue + uw + un + us - 4.0 * u) - lift * u_slope
            ret[1, k] = v + diffuse_rate * (ve + vw + vn + vs - 4.0 * v) - lift * v_slope
            ret[2, k] = warm - lift * warm_slope
            lifts[k] = lift
            eddy = eddy_base + eddy_slope * jnp.sqrt((xstretch - ystretch) ** 2 + (yshear + xshear) ** 2)
            mixing = mixing_base + mixing_slope * jnp.sqrt(u_slope**2 + v_slope**2) / (
                1.0 + stable_weight * jnp.maximum(warm_slope, 0.0)
            )
            height = jnp.exp(jnp.zeros((1, COLS), F32) + k.astype(F32) * (1.0 / level_decay))
            dens[k] = jnp.sqrt(warm) * height
            coef[0, k] = eddy - jnp.minimum(u, 0.0)
            coef[1, k] = eddy + jnp.maximum(u, 0.0)
            coef[2, k] = eddy - jnp.minimum(v, 0.0)
            coef[3, k] = eddy + jnp.maximum(v, 0.0)
            coef[4, k] = mixing - jnp.minimum(lift, 0.0)
            coef[5, k] = mixing + jnp.maximum(lift, 0.0)
            coef[6, k] = 1.0 - (jnp.abs(u) + jnp.abs(v) + jnp.abs(lift) + 4.0 * eddy + 2.0 * mixing)
        return total

    lax.fori_loop(0, G, diagnose, jnp.zeros((ROWS, COLS), F32))
    dens[NZ] = jnp.zeros((ROWS, COLS), F32)

    lift_back, back = [], []
    for d in range(1, G):
        peer = jnp.bitwise_xor(gx, d)
        if d % 4:
            copy = remote(
                lifts.at[LV * peer + 1 - peer % 2], lift_recv.at[own_x, own_z],
                lift_s.at[d], lift_r.at[d], (grp, peer, gy),
            )
            copy.start()
            lift_back.append(copy)
    for d in range(1, G):
        peer = jnp.bitwise_xor(gx, d)
        if d % 4:
            copy = remote(
                ret.at[:, LV * peer + peer % 2], met_out.at[:, peer % 2, own_x, own_z],
                ret_s.at[d], ret_r.at[d], (grp, peer, gy),
            )
        else:
            copy = remote(
                ret.at[:, pl.ds(LV * peer, LV)], met_out.at[:, :, own_x, own_z],
                ret_s.at[d], ret_r.at[d], (grp, peer, gy),
            )
        copy.start()
        back.append(copy)
    own_back = pltpu.make_async_copy(
        ret.at[:, own_levels], met_out.at[:, :, own_x, own_z], local.at[13]
    )
    own_back.start()

    pl.when(line > 0)(arows_up.wait_recv)
    pl.when(line < last_line)(arows_down.wait_recv)
    pl.when(gy > 0)(acols_up.wait_recv)
    pl.when(gy < GY - 1)(acols_down.wait_recv)

    speeds = [table_ref[class_ref[b]] for b in range(BINS)]

    def transport(k, _):
        up, down = jnp.minimum(k + 1, NZ - 1), jnp.maximum(k - 1, 0)
        for b in range(BINS):
            here = conc[b, k]
            at = (b % 4) * NZ + k
            east, west = along_x(
                here, arow_recv[0, b, pl.ds(k, 1), :], arow_recv[1, b, pl.ds(k, 1), :]
            )
            below = pltpu.roll(acol_recv[0, b // 4], lax.rem(128 - at, 128), 1)
            above = pltpu.roll(acol_recv[1, b // 4], 127 - at, 1)
            north, south = along_y(here, below, above)
            out = here * (coef[6, k] - speeds[b] * dens[k])
            out = out + conc[b, up] * (coef[4, k] + speeds[b] * dens[k + 1])
            out = out + east * coef[0, k] + west * coef[1, k]
            out = out + north * coef[2, k] + south * coef[3, k]
            ash_out[b, k] = out + conc[b, down] * coef[5, k]
        return 0

    lax.fori_loop(0, NZ, transport, 0)

    for copy in pairs + lift_back:
        copy.wait_recv()
    half = jnp.where(gx % 2 == 0, 0.5, -0.5).astype(F32)

    def step_rows(x, _):
        for j in range(1, 4):
            z = jnp.bitwise_xor(own_z, j)
            g = 4 * x + z
            edge_cols = edge_send[g, :, COLS : COLS + 128]
            lift = lift_recv[x, z]
            for f in range(3):
                field = met[f, mine, x, z]
                slope = half * (partner[f, x, z] - met[f, 1 - mine, x, z])
                after = field - lift * slope
                if f < 2:
                    at = 2 * f + mine
                    east, west = along_x(
                        field,
                        edge_send[g, pl.ds(at, 1), 0:COLS],
                        edge_send[g, pl.ds(at + 4, 1), 0:COLS],
                    )
                    below = jnp.concatenate(
                        [pltpu.roll(edge_cols, 128 - at, 1), pltpu.roll(edge_cols, 64 - at, 1)], axis=0
                    )
                    above = jnp.concatenate(
                        [pltpu.roll(edge_cols, 123 - at, 1), pltpu.roll(edge_cols, 59 - at, 1)], axis=0
                    )
                    north, south = along_y(field, below, above)
                    after = after + diffuse_rate * (east + west + north + south - 4.0 * field)
                met_out[f, mine, x, z] = after
        return 0

    lax.fori_loop(0, 4, step_rows, 0)

    for copy in back:
        copy.wait_recv()
    own_back.wait()
    for copy in bulk + pairs + edges + lift_back + back:
        copy.wait_send()
    pl.when(grp < GRP - 1)(rows_up.wait_send)
    pl.when(grp > 0)(rows_down.wait_send)
    pl.when(gy < GY - 1)(cols_up.wait_send)
    pl.when(gy > 0)(cols_down.wait_send)
    pl.when(line < last_line)(arows_up.wait_send)
    pl.when(line > 0)(arows_down.wait_send)
    pl.when(gy < GY - 1)(acols_up.wait_send)
    pl.when(gy > 0)(acols_down.wait_send)


def body(wind_u, wind_v, theta, ash, src_x, src_y, src_rate, settle_class, settle_table):
    hbm = pl.BlockSpec(memory_space=pltpu.HBM)
    vmem = pl.BlockSpec(memory_space=pltpu.VMEM)
    dma = pltpu.SemaphoreType.DMA
    tiled = (LV, 4, 4, ROWS, COLS)
    ash_next, met_next = pl.pallas_call(
            kernel,
            out_shape=(
                pltpu.VMEM((BINS, NZ, ROWS, COLS), F32),
                pltpu.VMEM((3,) + tiled, F32),
            ),
            in_specs=[hbm] * 9,
            out_specs=(vmem, vmem),
            scratch_shapes=[
                pltpu.SMEM((NSRC,), jnp.int32),
                pltpu.SMEM((NSRC,), jnp.int32),
                pltpu.SMEM((NSRC, BINS, NZ), F32),
                pltpu.SMEM(settle_class.shape, jnp.int32),
                pltpu.SMEM(settle_table.shape, F32),
                pltpu.VMEM((3,) + tiled, F32),
                pltpu.VMEM((3,) + tiled[1:], F32),
                pltpu.VMEM(tiled[1:], F32),
                pltpu.VMEM((3, NZ, ROWS, COLS), F32),
                pltpu.VMEM((BINS, NZ, ROWS, COLS), F32),
                pltpu.VMEM((3, NZ, ROWS, COLS), F32),
                pltpu.VMEM((NZ, ROWS, COLS), F32),
                pltpu.VMEM((7, NZ, ROWS, COLS), F32),
                pltpu.VMEM((NZ + 1, ROWS, COLS), F32),
                pltpu.VMEM((NSRC, ROWS, COLS), F32),
                pltpu.VMEM((2, 8, COLS), F32),
                pltpu.VMEM((2, 8, COLS), F32),
                pltpu.VMEM((2, G, 8, 128), F32),
                pltpu.VMEM((2, G, 8, 128), F32),
                pltpu.VMEM((G, 8, COLS + 128), F32),
                pltpu.VMEM((G, 8, COLS + 128), F32),
                pltpu.VMEM((2, BINS, NZ, COLS), F32),
                pltpu.VMEM((2, BINS, NZ, COLS), F32),
                pltpu.VMEM((2, 2, ROWS, 128), F32),
                pltpu.VMEM((2, 2, ROWS, 128), F32),
                dma((3, G)), dma((3, G)),
                dma((G,)), dma((G,)),
                dma((G,)), dma((G,)),
                dma((G,)), dma((G,)),
                dma((3, 4)), dma((3, 4)),
                dma((8,)), dma((8,)),
                dma((14,)),
            ],
            compiler_params=pltpu.CompilerParams(
                collective_id=0, has_side_effects=True, vmem_limit_bytes=48 * 2**20
            ),
    )(
        *(
            pltpu.with_memory_space_constraint(array, pltpu.HBM)
            for array in (
                wind_u.reshape(tiled), wind_v.reshape(tiled), theta.reshape(tiled), ash,
                src_x, src_y, src_rate, settle_class, settle_table,
            )
        )
    )
    return ash_next, met_next.reshape(3, LV, MROWS, COLS)


def solution(mesh):
    in_specs = (
        P("gx", "grp", "gy"),
        P("gx", "grp", "gy"),
        P("gx", "grp", "gy"),
        P(None, None, ("grp", "gx"), "gy"),
        P(),
        P(),
        P(),
        P(),
        P(),
    )
    out_specs = (P(None, None, ("grp", "gx"), "gy"), P(None, "gx", "grp", "gy"))
    return jax.shard_map(body, mesh=mesh, in_specs=in_specs, out_specs=out_specs, check_vma=False)
```

```python
import functools

import jax
import jax.numpy as jnp
from jax import lax
from jax.experimental import pallas as pl
from jax.experimental.pallas import tpu as pltpu
from jax.sharding import PartitionSpec as P

MESH = pl.DeviceIdType.MESH
F32 = jnp.float32

diffuse_rate = 0.1
lift_scale = 0.1
lift_limit = 0.15
eddy_base = 0.005
eddy_slope = 0.03
mixing_base = 0.005
mixing_slope = 0.08
stable_weight = 20.0
level_decay = 32.0

G = 16
GRP = 4
GY = 4
LV = 2
NZ = 32
ROWS = 16
COLS = 256
MROWS = 256
BINS = 8
NSRC = 16


def kernel(
    u_ref, v_ref, t_ref, ash_ref, sx_hbm, sy_hbm, rate_hbm, class_hbm, table_hbm,
    ash_out, met_out,
    sx_ref, sy_ref, rate_ref, class_ref, table_ref,
    met, partner, cum_recv, fields, conc, ret, cums, coef, dens, marks,
    row_send, row_recv, col_send, col_recv, edge_send, edge_recv,
    arow_send, arow_recv, acol_send, acol_recv,
    bulk_s, bulk_r, edge_s, edge_r, ret_s, ret_r, cum_s, cum_r, mate_s, mate_r, part_s, part_r, near_s, near_r, local,
):
    grp, gx, gy = lax.axis_index("grp"), lax.axis_index("gx"), lax.axis_index("gy")
    line = grp * G + gx
    last_line = GRP * G - 1
    wrap_up, wrap_down = gx == G - 1, gx == 0
    row_up = (grp + wrap_up.astype(jnp.int32), lax.rem(gx + 1, G), gy)
    row_down = (grp - wrap_down.astype(jnp.int32), lax.rem(gx + G - 1, G), gy)

    sources = (u_ref, v_ref, t_ref)
    met_in = [pltpu.make_async_copy(sources[f], met.at[f], local.at[f]) for f in range(3)]
    ash_in = pltpu.make_async_copy(ash_ref, conc, local.at[3])
    small_in = [
        pltpu.make_async_copy(src, dst, local.at[8 + i])
        for i, (src, dst) in enumerate(
            (
                (sx_hbm, sx_ref), (sy_hbm, sy_ref), (rate_hbm, rate_ref),
                (class_hbm, class_ref), (table_hbm, table_ref),
            )
        )
    ]
    for copy in met_in + [ash_in] + small_in:
        copy.start()

    barrier = pltpu.get_barrier_semaphore()

    def greet(device):
        pl.semaphore_signal(barrier, inc=1, device_id=device, device_id_type=MESH)

    for d in range(G - 1, 0, -1):
        greet((grp, jnp.bitwise_xor(gx, d), gy))
    pl.when(gy > 0)(lambda: greet((grp, gx, gy - 1)))
    pl.when(gy < GY - 1)(lambda: greet((grp, gx, gy + 1)))
    pl.when(grp > 0)(lambda: greet((grp - 1, gx, gy)))
    pl.when(grp < GRP - 1)(lambda: greet((grp + 1, gx, gy)))
    far_down = jnp.logical_and(wrap_down, grp > 0)
    far_up = jnp.logical_and(wrap_up, grp < GRP - 1)
    pl.when(far_down)(lambda: greet(row_down))
    pl.when(far_up)(lambda: greet(row_up))
    count = (
        G - 1
        + (gy > 0).astype(jnp.int32) + (gy < GY - 1).astype(jnp.int32)
        + (grp > 0).astype(jnp.int32) + (grp < GRP - 1).astype(jnp.int32)
        + far_down.astype(jnp.int32) + far_up.astype(jnp.int32)
    )
    pl.semaphore_wait(barrier, count)

    def remote(src, dst, send, recv, device):
        return pltpu.make_async_remote_copy(
            src_ref=src, dst_ref=dst, send_sem=send, recv_sem=recv,
            device_id=device, device_id_type=MESH,
        )

    own_levels = pl.ds(LV * gx, LV)
    own_x, own_z = gx // 4, gx % 4
    bulk = []
    for d in range(1, G):
        peer = jnp.bitwise_xor(gx, d)
        for f in range(3):
            copy = remote(
                sources[f].at[:, peer // 4, peer % 4], fields.at[f, own_levels],
                bulk_s.at[f, d], bulk_r.at[f, d], (grp, peer, gy),
            )
            copy.start()
            bulk.append(copy)
    own_bulk = []
    for f in range(3):
        copy = pltpu.make_async_copy(
            sources[f].at[:, own_x, own_z], fields.at[f, own_levels], local.at[4 + f]
        )
        copy.start()
        own_bulk.append(copy)

    mine = 1 - gx % 2
    mate = jnp.bitwise_xor(gx, 1)
    pairs = []
    for j in range(2, 4):
        group = jnp.bitwise_xor(mate % 4, j)
        for f in range(3):
            copy = remote(
                sources[f].at[mine, :, group], partner.at[f, :, group],
                part_s.at[f, j], part_r.at[f, j], (grp, mate, gy),
            )
            pairs.append(copy)

    lane = lax.broadcasted_iota(jnp.int32, (8, 128), 1)
    for copy in met_in:
        copy.wait()
    for f in range(2):
        for lev in range(LV):
            at = 2 * f + lev
            row_send[0, at : at + 1, :] = met[f, lev, 3, 3, ROWS - 1 : ROWS, :]
            row_send[1, at : at + 1, :] = met[f, lev, 0, 0, 0:1, :]
    row_send[0, 4:8, :] = jnp.zeros((4, COLS), F32)
    row_send[1, 4:8, :] = jnp.zeros((4, COLS), F32)

    def pack_columns(g, _):
        right = jnp.zeros((8, 128), F32)
        left = jnp.zeros((8, 128), F32)
        for half in range(2):
            rows = slice(8 * half, 8 * half + 8)
            for f in range(2):
                for lev in range(LV):
                    c = 64 * half + 2 * f + lev
                    tail = met[f, lev, g // 4, g % 4, rows, 128:256]
                    right = jnp.where(lane == c, pltpu.roll(tail, c + 1, 1), right)
                    head = met[f, lev, g // 4, g % 4, rows, 0:128]
                    left = jnp.where(lane == c + 4, pltpu.roll(head, c + 4, 1), left)
        col_send[0, g] = right
        col_send[1, g] = left
        return 0

    lax.fori_loop(0, G, pack_columns, 0)

    rows_up = remote(row_send.at[0], row_recv.at[0], near_s.at[0], near_r.at[0], (grp + 1, gx, gy))
    rows_down = remote(row_send.at[1], row_recv.at[1], near_s.at[1], near_r.at[1], (grp - 1, gx, gy))
    cols_up = remote(col_send.at[0], col_recv.at[0], near_s.at[2], near_r.at[2], (grp, gx, gy + 1))
    cols_down = remote(col_send.at[1], col_recv.at[1], near_s.at[3], near_r.at[3], (grp, gx, gy - 1))

    def clear(ref):
        ref[...] = jnp.zeros(ref.shape, F32)

    pl.when(gy < GY - 1)(cols_up.start)
    pl.when(gy > 0)(cols_down.start)
    pl.when(grp < GRP - 1)(rows_up.start)
    pl.when(grp > 0)(rows_down.start)
    pl.when(grp == 0)(lambda: clear(row_recv.at[0]))
    pl.when(grp == GRP - 1)(lambda: clear(row_recv.at[1]))
    pl.when(gy == 0)(lambda: clear(col_recv.at[0]))
    pl.when(gy == GY - 1)(lambda: clear(col_recv.at[1]))

    def pack_rows(g, _):
        before, after = jnp.maximum(g - 1, 0), jnp.minimum(g + 1, G - 1)
        for f in range(2):
            for lev in range(LV):
                at = 2 * f + lev
                edge_send[g, at : at + 1, 0:COLS] = met[f, lev, before // 4, before % 4, ROWS - 1 : ROWS, :]
                edge_send[g, at + 4 : at + 5, 0:COLS] = met[f, lev, after // 4, after % 4, 0:1, :]
        return 0

    lax.fori_loop(0, G, pack_rows, 0)
    pl.when(grp > 0)(rows_up.wait_recv)
    pl.when(grp < GRP - 1)(rows_down.wait_recv)
    pl.when(gy > 0)(cols_up.wait_recv)
    pl.when(gy < GY - 1)(cols_down.wait_recv)
    edge_send[0, 0:4, 0:COLS] = row_recv[0, 0:4, :]
    edge_send[G - 1, 4:8, 0:COLS] = row_recv[1, 0:4, :]

    def merge_columns(g, _):
        edge_send[g, :, COLS : COLS + 128] = jnp.where(
            lane % 64 < 4, col_recv[0, g], col_recv[1, g]
        )
        return 0

    lax.fori_loop(0, G, merge_columns, 0)
    edges = []
    for d in range(1, G):
        peer = jnp.bitwise_xor(gx, d)
        copy = remote(
            edge_send.at[peer], edge_recv.at[gx], edge_s.at[d], edge_r.at[d], (grp, peer, gy)
        )
        copy.start()
        edges.append(copy)
    own_edge = pltpu.make_async_copy(edge_send.at[gx], edge_recv.at[gx], local.at[7])
    own_edge.start()

    row16 = lax.broadcasted_iota(jnp.int32, (ROWS, COLS), 0)
    lane16 = lax.broadcasted_iota(jnp.int32, (ROWS, COLS), 1)
    start_x, start_y = line * ROWS, gy * COLS

    for copy in small_in:
        copy.wait()

    def mark(s, _):
        hit = jnp.logical_and(row16 == sx_ref[s] - start_x, lane16 == sy_ref[s] - start_y)
        marks[s] = jnp.where(hit, 1.0, 0.0).astype(F32)
        return 0

    lax.fori_loop(0, NSRC, mark, 0)
    ash_in.wait()

    def emit(k, _):
        for b in range(BINS):
            total = conc[b, k]
            for s in range(NSRC):
                total = total + marks[s] * rate_ref[s, b, k]
            conc[b, k] = total
        return 0

    lax.fori_loop(0, NZ, emit, 0)

    lane128 = lax.broadcasted_iota(jnp.int32, (ROWS, 128), 1)

    def pack_ash(k, sums):
        sums = list(sums)
        for b in range(BINS):
            slab = conc[b, k]
            arow_send[0, b, pl.ds(k, 1), :] = slab[ROWS - 1 : ROWS]
            arow_send[1, b, pl.ds(k, 1), :] = slab[0:1]
            at = (b % 4) * NZ + k
            spot = lane128 == at
            right = pltpu.roll(slab[:, 128:256], lax.rem(at + 1, 128), 1)
            left = pltpu.roll(slab[:, 0:128], at, 1)
            sums[b // 4] = jnp.where(spot, right, sums[b // 4])
            sums[2 + b // 4] = jnp.where(spot, left, sums[2 + b // 4])
        return tuple(sums)

    packed = lax.fori_loop(0, NZ, pack_ash, tuple(jnp.zeros((ROWS, 128), F32) for _ in range(4)))
    for side in range(2):
        for part in range(2):
            acol_send[side, part] = packed[2 * side + part]

    arows_up = remote(arow_send.at[0], arow_recv.at[0], near_s.at[4], near_r.at[4], row_up)
    arows_down = remote(arow_send.at[1], arow_recv.at[1], near_s.at[5], near_r.at[5], row_down)
    acols_up = remote(acol_send.at[0], acol_recv.at[0], near_s.at[6], near_r.at[6], (grp, gx, gy + 1))
    acols_down = remote(acol_send.at[1], acol_recv.at[1], near_s.at[7], near_r.at[7], (grp, gx, gy - 1))
    pl.when(line < last_line)(arows_up.start)
    pl.when(line > 0)(arows_down.start)
    pl.when(gy < GY - 1)(acols_up.start)
    pl.when(gy > 0)(acols_down.start)
    pl.when(line == 0)(lambda: clear(arow_recv.at[0]))
    pl.when(line == last_line)(lambda: clear(arow_recv.at[1]))
    pl.when(gy == 0)(lambda: clear(acol_recv.at[0]))
    pl.when(gy == GY - 1)(lambda: clear(acol_recv.at[1]))

    for copy in bulk:
        copy.wait_send()
    for copy in pairs:
        copy.start()
    for copy in bulk:
        copy.wait_recv()
    for copy in edges:
        copy.wait_recv()
    for copy in own_bulk:
        copy.wait()
    own_edge.wait()

    first_row, end_row = row16 == 0, row16 == ROWS - 1
    first_lane, end_lane = lane16 == 0, lane16 == COLS - 1

    def twice(half):
        return jnp.concatenate([half, half], axis=1)

    def along_x(field, below, above):
        east = jnp.where(end_row, above, pltpu.roll(field, ROWS - 1, 0))
        west = jnp.where(first_row, below, pltpu.roll(field, 1, 0))
        return east, west

    def along_y(field, below, above):
        north = jnp.where(end_lane, twice(above), pltpu.roll(field, COLS - 1, 1))
        south = jnp.where(first_lane, twice(below), pltpu.roll(field, 1, 1))
        return north, south

    def diagnose(g, total):
        edge_cols = edge_recv[g, :, COLS : COLS + 128]
        for lev in range(LV):
            k = LV * g + lev
            up, down = jnp.minimum(k + 1, NZ - 1), jnp.maximum(k - 1, 0)
            wind = []
            for f in range(2):
                at = 2 * f + lev
                field = fields[f, k]
                east, west = along_x(
                    field,
                    edge_recv[g, at : at + 1, 0:COLS],
                    edge_recv[g, at + 4 : at + 5, 0:COLS],
                )
                below = jnp.concatenate(
                    [pltpu.roll(edge_cols, (128 - at) % 128, 1), pltpu.roll(edge_cols, 64 - at, 1)], axis=0
                )
                above = jnp.concatenate(
                    [pltpu.roll(edge_cols, 127 - at - 4, 1), pltpu.roll(edge_cols, 63 - at - 4, 1)], axis=0
                )
                north, south = along_y(field, below, above)
                slope = 0.5 * (fields[f, up] - fields[f, down])
                wind.append((field, east, west, north, south, slope))
            warm = fields[2, k]
            warm_slope = 0.5 * (fields[2, up] - fields[2, down])
            (u, ue, uw, un, us, u_slope), (v, ve, vw, vn, vs, v_slope) = wind
            xstretch, yshear = 0.5 * (ue - uw), 0.5 * (un - us)
            xshear, ystretch = 0.5 * (ve - vw), 0.5 * (vn - vs)
            total = total + (xstretch + ystretch)
            lift = jnp.clip(-lift_scale * total, -lift_limit, lift_limit)
            ret[0, k] = u + diffuse_rate * (ue + uw + un + us - 4.0 * u) - lift * u_slope
            ret[1, k] = v + diffuse_rate * (ve + vw + vn + vs - 4.0 * v) - lift * v_slope
            ret[2, k] = warm - lift * warm_slope
            if lev == 1:
                cums[g] = total
            eddy = eddy_base + eddy_slope * jnp.sqrt((xstretch - ystretch) ** 2 + (yshear + xshear) ** 2)
            mixing = mixing_base + mixing_slope * jnp.sqrt(u_slope**2 + v_slope**2) / (
                1.0 + stable_weight * jnp.maximum(warm_slope, 0.0)
            )
            height = jnp.exp(jnp.zeros((1, COLS), F32) + k.astype(F32) * (1.0 / level_decay))
            dens[k] = jnp.sqrt(warm) * height
            coef[0, k] = eddy - jnp.minimum(u, 0.0)
            coef[1, k] = eddy + jnp.maximum(u, 0.0)
            coef[2, k] = eddy - jnp.minimum(v, 0.0)
            coef[3, k] = eddy + jnp.maximum(v, 0.0)
            coef[4, k] = mixing - jnp.minimum(lift, 0.0)
            coef[5, k] = mixing + jnp.maximum(lift, 0.0)
            coef[6, k] = 1.0 - (jnp.abs(u) + jnp.abs(v) + jnp.abs(lift) + 4.0 * eddy + 2.0 * mixing)
        return total

    lax.fori_loop(0, G, diagnose, jnp.zeros((ROWS, COLS), F32))
    dens[NZ] = jnp.zeros((ROWS, COLS), F32)

    near = jnp.logical_or(own_z == 1, own_z == 2)
    near_z = jnp.where(own_z < 2, 2, 1)
    half_z = jnp.where(own_z < 2, 2, 0)
    cum_back = []
    for dx in range(4):
        peer = 4 * jnp.bitwise_xor(own_x, dx) + near_z
        copy = remote(
            cums.at[2 * (peer // 2)], cum_recv.at[own_x, own_z],
            cum_s.at[dx], cum_r.at[own_z % 2, dx], (grp, peer, gy),
        )
        copy.start()
        cum_back.append(copy)
    back = []
    for d in range(1, G):
        peer = jnp.bitwise_xor(gx, d)
        if d % 4 > 1:
            copy = remote(
                ret.at[:, LV * peer + peer % 2], met_out.at[:, peer % 2, own_x, own_z],
                ret_s.at[d], ret_r.at[d], (grp, peer, gy),
            )
        else:
            copy = remote(
                ret.at[:, pl.ds(LV * peer, LV)], met_out.at[:, :, own_x, own_z],
                ret_s.at[d], ret_r.at[d], (grp, peer, gy),
            )
        copy.start()
        back.append(copy)
    own_back = pltpu.make_async_copy(
        ret.at[:, own_levels], met_out.at[:, :, own_x, own_z], local.at[13]
    )
    own_back.start()

    pl.when(line > 0)(arows_up.wait_recv)
    pl.when(line < last_line)(arows_down.wait_recv)
    pl.when(gy > 0)(acols_up.wait_recv)
    pl.when(gy < GY - 1)(acols_down.wait_recv)

    speeds = [table_ref[class_ref[b]] for b in range(BINS)]

    def transport(k, _):
        up, down = jnp.minimum(k + 1, NZ - 1), jnp.maximum(k - 1, 0)
        for b in range(BINS):
            here = conc[b, k]
            at = (b % 4) * NZ + k
            east, west = along_x(
                here, arow_recv[0, b, pl.ds(k, 1), :], arow_recv[1, b, pl.ds(k, 1), :]
            )
            below = pltpu.roll(acol_recv[0, b // 4], lax.rem(128 - at, 128), 1)
            above = pltpu.roll(acol_recv[1, b // 4], 127 - at, 1)
            north, south = along_y(here, below, above)
            out = here * (coef[6, k] - speeds[b] * dens[k])
            out = out + conc[b, up] * (coef[4, k] + speeds[b] * dens[k + 1])
            out = out + east * coef[0, k] + west * coef[1, k]
            out = out + north * coef[2, k] + south * coef[3, k]
            ash_out[b, k] = out + conc[b, down] * coef[5, k]
        return 0

    lax.fori_loop(0, NZ, transport, 0)

    hand_on = remote(
        cum_recv.at[:, pl.ds(half_z, 2)], cum_recv.at[:, pl.ds(half_z, 2)],
        mate_s.at[0], mate_r.at[0], (grp, mate, gy),
    )

    @pl.when(near)
    def _():
        for parity in range(2):
            for dx in range(4):
                remote(
                    cums.at[0], cum_recv.at[own_x, own_z], cum_s.at[dx], cum_r.at[parity, dx], (grp, mate, gy)
                ).wait_recv()
        hand_on.start()

    pl.when(jnp.logical_not(near))(hand_on.wait_recv)
    for copy in pairs:
        copy.wait_recv()
    half = jnp.where(gx % 2 == 0, 0.5, -0.5).astype(F32)
    above_cum = (gx % 2).astype(F32)

    def step_rows(x, _):
        for j in range(2, 4):
            z = jnp.bitwise_xor(own_z, j)
            g = 4 * x + z
            edge_cols = edge_send[g, :, COLS : COLS + 128]
            wind = []
            for f in range(2):
                field = met[f, mine, x, z]
                at = 2 * f + mine
                east, west = along_x(
                    field,
                    edge_send[g, pl.ds(at, 1), 0:COLS],
                    edge_send[g, pl.ds(at + 4, 1), 0:COLS],
                )
                below = jnp.concatenate(
                    [pltpu.roll(edge_cols, 128 - at, 1), pltpu.roll(edge_cols, 64 - at, 1)], axis=0
                )
                above = jnp.concatenate(
                    [pltpu.roll(edge_cols, 123 - at, 1), pltpu.roll(edge_cols, 59 - at, 1)], axis=0
                )
                north, south = along_y(field, below, above)
                wind.append((east, west, north, south))
            (ue, uw, un, us), (ve, vw, vn, vs) = wind
            total = cum_recv[x, z] + above_cum * (0.5 * (ue - uw) + 0.5 * (vn - vs))
            lift = jnp.clip(-lift_scale * total, -lift_limit, lift_limit)
            for f in range(3):
                field = met[f, mine, x, z]
                slope = half * (partner[f, x, z] - met[f, 1 - mine, x, z])
                after = field - lift * slope
                if f < 2:
                    after = after + diffuse_rate * (sum(wind[f][1:], wind[f][0]) - 4.0 * field)
                met_out[f, mine, x, z] = after
        return 0

    lax.fori_loop(0, 4, step_rows, 0)

    for copy in back:
        copy.wait_recv()
    own_back.wait()
    for copy in pairs + edges + cum_back + back:
        copy.wait_send()
    pl.when(near)(hand_on.wait_send)
    pl.when(grp < GRP - 1)(rows_up.wait_send)
    pl.when(grp > 0)(rows_down.wait_send)
    pl.when(gy < GY - 1)(cols_up.wait_send)
    pl.when(gy > 0)(cols_down.wait_send)
    pl.when(line < last_line)(arows_up.wait_send)
    pl.when(line > 0)(arows_down.wait_send)
    pl.when(gy < GY - 1)(acols_up.wait_send)
    pl.when(gy > 0)(acols_down.wait_send)


def write_out(ash_ref, met_ref, ash_out, met_out, done):
    copies = [pltpu.make_async_copy(ash_ref.at[b], ash_out.at[b], done.at[b]) for b in range(BINS)]
    copies += [
        pltpu.make_async_copy(met_ref.at[f], met_out.at[f], done.at[BINS + f]) for f in range(3)
    ]
    for copy in copies:
        copy.start()
    for copy in copies:
        copy.wait()


def body(wind_u, wind_v, theta, ash, src_x, src_y, src_rate, settle_class, settle_table):
    hbm = pl.BlockSpec(memory_space=pltpu.HBM)
    vmem = pl.BlockSpec(memory_space=pltpu.VMEM)
    dma = pltpu.SemaphoreType.DMA
    tiled = (LV, 4, 4, ROWS, COLS)
    ash_next, met_next = pl.pallas_call(
            kernel,
            out_shape=(
                pltpu.VMEM((BINS, NZ, ROWS, COLS), F32),
                pltpu.VMEM((3,) + tiled, F32),
            ),
            in_specs=[hbm] * 9,
            out_specs=(vmem, vmem),
            scratch_shapes=[
                pltpu.SMEM((NSRC,), jnp.int32),
                pltpu.SMEM((NSRC,), jnp.int32),
                pltpu.SMEM((NSRC, BINS, NZ), F32),
                pltpu.SMEM(settle_class.shape, jnp.int32),
                pltpu.SMEM(settle_table.shape, F32),
                pltpu.VMEM((3,) + tiled, F32),
                pltpu.VMEM((3,) + tiled[1:], F32),
                pltpu.VMEM(tiled[1:], F32),
                pltpu.VMEM((3, NZ, ROWS, COLS), F32),
                pltpu.VMEM((BINS, NZ, ROWS, COLS), F32),
                pltpu.VMEM((3, NZ, ROWS, COLS), F32),
                pltpu.VMEM((G, ROWS, COLS), F32),
                pltpu.VMEM((7, NZ, ROWS, COLS), F32),
                pltpu.VMEM((NZ + 1, ROWS, COLS), F32),
                pltpu.VMEM((NSRC, ROWS, COLS), F32),
                pltpu.VMEM((2, 8, COLS), F32),
                pltpu.VMEM((2, 8, COLS), F32),
                pltpu.VMEM((2, G, 8, 128), F32),
                pltpu.VMEM((2, G, 8, 128), F32),
                pltpu.VMEM((G, 8, COLS + 128), F32),
                pltpu.VMEM((G, 8, COLS + 128), F32),
                pltpu.VMEM((2, BINS, NZ, COLS), F32),
                pltpu.VMEM((2, BINS, NZ, COLS), F32),
                pltpu.VMEM((2, 2, ROWS, 128), F32),
                pltpu.VMEM((2, 2, ROWS, 128), F32),
                dma((3, G)), dma((3, G)),
                dma((G,)), dma((G,)),
                dma((G,)), dma((G,)),
                dma((4,)), dma((2, 4)),
                dma((1,)), dma((1,)),
                dma((3, 4)), dma((3, 4)),
                dma((8,)), dma((8,)),
                dma((14,)),
            ],
            compiler_params=pltpu.CompilerParams(
                collective_id=0, has_side_effects=True, vmem_limit_bytes=48 * 2**20
            ),
    )(
        *(
            pltpu.with_memory_space_constraint(array, pltpu.HBM)
            for array in (
                wind_u.reshape(tiled), wind_v.reshape(tiled), theta.reshape(tiled), ash,
                src_x, src_y, src_rate, settle_class, settle_table,
            )
        )
    )
    ash_next, met_next = pl.pallas_call(
        write_out,
        out_shape=(
            pltpu.HBM((BINS, NZ, ROWS, COLS), F32),
            pltpu.HBM((3,) + tiled, F32),
        ),
        in_specs=[vmem, vmem],
        out_specs=(hbm, hbm),
        scratch_shapes=[dma((BINS + 3,))],
        compiler_params=pltpu.CompilerParams(vmem_limit_bytes=2**20),
    )(
        pltpu.with_memory_space_constraint(ash_next, pltpu.VMEM),
        pltpu.with_memory_space_constraint(met_next, pltpu.VMEM),
    )
    return ash_next, met_next.reshape(3, LV, MROWS, COLS)


def solution(mesh):
    in_specs = (
        P("gx", "grp", "gy"),
        P("gx", "grp", "gy"),
        P("gx", "grp", "gy"),
        P(None, None, ("grp", "gx"), "gy"),
        P(),
        P(),
        P(),
        P(),
        P(),
    )
    out_specs = (P(None, None, ("grp", "gx"), "gy"), P(None, "gx", "grp", "gy"))
    return jax.shard_map(body, mesh=mesh, in_specs=in_specs, out_specs=out_specs, check_vma=False)
```

```python
import functools

import jax
import jax.numpy as jnp
from jax import lax
from jax.experimental import pallas as pl
from jax.experimental.pallas import tpu as pltpu
from jax.sharding import PartitionSpec as P

MESH = pl.DeviceIdType.MESH
F32 = jnp.float32

diffuse_rate = 0.1
lift_scale = 0.1
lift_limit = 0.15
eddy_base = 0.005
eddy_slope = 0.03
mixing_base = 0.005
mixing_slope = 0.08
stable_weight = 20.0
level_decay = 32.0

G = 16
GRP = 4
GY = 4
LV = 2
NZ = 32
ROWS = 16
COLS = 256
MROWS = 256
BINS = 8
NSRC = 16


def kernel(
    u_ref, v_ref, t_ref, ash_ref, sx_hbm, sy_hbm, rate_hbm, class_hbm, table_hbm,
    ash_out, met_out,
    sx_ref, sy_ref, rate_ref, class_ref, table_ref,
    met, partner, cum_recv, fields, conc, ret, cums, coef, dens, marks,
    row_send, row_recv, col_send, col_recv, edge_send, edge_recv,
    arow_send, arow_recv, acol_send, acol_recv, tcol_send, tcol_recv,
    bulk_s, bulk_r, edge_s, edge_r, ret_s, ret_r, cum_s, cum_r, mate_s, mate_r, part_s, part_r, near_s, near_r, local, ready,
):
    grp, gx, gy = lax.axis_index("grp"), lax.axis_index("gx"), lax.axis_index("gy")
    line = grp * G + gx
    last_line = GRP * G - 1
    wrap_up, wrap_down = gx == G - 1, gx == 0
    row_up = (grp + wrap_up.astype(jnp.int32), lax.rem(gx + 1, G), gy)
    row_down = (grp - wrap_down.astype(jnp.int32), lax.rem(gx + G - 1, G), gy)

    sources = (u_ref, v_ref, t_ref)
    met_in = [pltpu.make_async_copy(sources[f], met.at[f], local.at[f]) for f in range(3)]
    ash_in = pltpu.make_async_copy(ash_ref, conc, local.at[3])
    small_in = [
        pltpu.make_async_copy(src, dst, local.at[8 + i])
        for i, (src, dst) in enumerate(
            (
                (sx_hbm, sx_ref), (sy_hbm, sy_ref), (rate_hbm, rate_ref),
                (class_hbm, class_ref), (table_hbm, table_ref),
            )
        )
    ]

    barrier = pltpu.get_barrier_semaphore()

    def greet(device):
        pl.semaphore_signal(barrier, inc=1, device_id=device, device_id_type=MESH)

    for d in range(G - 1, 0, -1):
        greet((grp, jnp.bitwise_xor(gx, d), gy))
    pl.when(gy > 0)(lambda: greet((grp, gx, gy - 1)))
    pl.when(gy < GY - 1)(lambda: greet((grp, gx, gy + 1)))
    pl.when(jnp.logical_or(grp == 1, grp == 3))(lambda: greet((grp - 1, gx, gy)))
    pl.when(grp < GRP - 1)(lambda: greet((grp + 1, gx, gy)))
    far_down = jnp.logical_and(wrap_down, grp > 0)
    far_up = jnp.logical_and(wrap_up, grp < GRP - 1)
    pl.when(jnp.logical_and(far_down, grp != 2))(lambda: greet(row_down))
    pl.when(far_up)(lambda: greet(row_up))
    count = (
        G - 1
        + (gy > 0).astype(jnp.int32) + (gy < GY - 1).astype(jnp.int32)
        + (grp > 0).astype(jnp.int32) + (grp % 2 == 0).astype(jnp.int32)
        + far_down.astype(jnp.int32) + jnp.logical_and(far_up, grp != 1).astype(jnp.int32)
    )
    for copy in met_in:
        copy.start()
    pl.semaphore_wait(barrier, count)

    def tell(index, device):
        pl.semaphore_signal(ready.at[index], inc=1, device_id=device, device_id_type=MESH)

    pl.when(grp == 2)(lambda: tell(0, (grp - 1, gx, gy)))
    pl.when(jnp.logical_and(grp == 2, wrap_down))(lambda: tell(1, row_down))

    def remote(src, dst, send, recv, device):
        return pltpu.make_async_remote_copy(
            src_ref=src, dst_ref=dst, send_sem=send, recv_sem=recv,
            device_id=device, device_id_type=MESH,
        )

    own_levels = pl.ds(LV * gx, LV)
    own_x, own_z = gx // 4, gx % 4
    for copy in met_in:
        copy.wait()
    bulk = []
    for d in range(1, G):
        peer = jnp.bitwise_xor(gx, d)
        copy = remote(
            met.at[:, :, peer // 4, peer % 4], fields.at[:, own_levels],
            bulk_s.at[d], bulk_r.at[d], (grp, peer, gy),
        )
        copy.start()
        bulk.append(copy)
    own_bulk = [
        pltpu.make_async_copy(met.at[:, :, own_x, own_z], fields.at[:, own_levels], local.at[4])
    ]
    own_bulk[0].start()
    for copy in small_in + [ash_in]:
        copy.start()

    mine = 1 - gx % 2
    mate = jnp.bitwise_xor(gx, 1)
    pairs = []
    for j in range(2, 4):
        group = jnp.bitwise_xor(mate % 4, j)
        pairs.append(
            remote(
                met.at[:, mine, :, group], partner.at[:, :, group],
                part_s.at[j], part_r.at[j], (grp, mate, gy),
            )
        )

    lane = lax.broadcasted_iota(jnp.int32, (8, 128), 1)
    for f in range(2):
        for lev in range(LV):
            at = 2 * f + lev
            row_send[0, at : at + 1, :] = met[f, lev, 3, 3, ROWS - 1 : ROWS, :]
            row_send[1, at : at + 1, :] = met[f, lev, 0, 0, 0:1, :]
    row_send[0, 4:8, :] = jnp.zeros((4, COLS), F32)
    row_send[1, 4:8, :] = jnp.zeros((4, COLS), F32)

    def pack_columns(g, _):
        right = jnp.zeros((8, 128), F32)
        left = jnp.zeros((8, 128), F32)
        for half in range(2):
            rows = slice(8 * half, 8 * half + 8)
            for f in range(2):
                for lev in range(LV):
                    c = 64 * half + 2 * f + lev
                    tail = met[f, lev, g // 4, g % 4, rows, 128:256]
                    right = jnp.where(lane == c, pltpu.roll(tail, c + 1, 1), right)
                    head = met[f, lev, g // 4, g % 4, rows, 0:128]
                    left = jnp.where(lane == c + 4, pltpu.roll(head, c + 4, 1), left)
        col_send[0, g] = right
        col_send[1, g] = left
        return 0

    lax.fori_loop(0, G, pack_columns, 0)

    rows_up = remote(row_send.at[0], row_recv.at[0], near_s.at[0], near_r.at[0], (grp + 1, gx, gy))
    rows_down = remote(row_send.at[1], row_recv.at[1], near_s.at[1], near_r.at[1], (grp - 1, gx, gy))
    cols_up = remote(col_send.at[0], col_recv.at[0], near_s.at[2], near_r.at[2], (grp, gx, gy + 1))
    cols_down = remote(col_send.at[1], col_recv.at[1], near_s.at[3], near_r.at[3], (grp, gx, gy - 1))

    def clear(ref):
        ref[...] = jnp.zeros(ref.shape, F32)

    pl.when(gy < GY - 1)(cols_up.start)
    pl.when(gy > 0)(cols_down.start)
    pl.when(grp == 1)(lambda: pl.semaphore_wait(ready.at[0], 1))
    pl.when(grp < GRP - 1)(rows_up.start)
    pl.when(grp > 0)(rows_down.start)
    pl.when(grp == 0)(lambda: clear(row_recv.at[0]))
    pl.when(grp == GRP - 1)(lambda: clear(row_recv.at[1]))
    pl.when(gy == 0)(lambda: clear(col_recv.at[0]))
    pl.when(gy == GY - 1)(lambda: clear(col_recv.at[1]))

    def pack_rows(g, _):
        before, after = jnp.maximum(g - 1, 0), jnp.minimum(g + 1, G - 1)
        for f in range(2):
            for lev in range(LV):
                at = 2 * f + lev
                edge_send[g, at : at + 1, 0:COLS] = met[f, lev, before // 4, before % 4, ROWS - 1 : ROWS, :]
                edge_send[g, at + 4 : at + 5, 0:COLS] = met[f, lev, after // 4, after % 4, 0:1, :]
        return 0

    lax.fori_loop(0, G, pack_rows, 0)
    pl.when(grp > 0)(rows_up.wait_recv)
    pl.when(grp < GRP - 1)(rows_down.wait_recv)
    pl.when(gy > 0)(cols_up.wait_recv)
    pl.when(gy < GY - 1)(cols_down.wait_recv)
    edge_send[0, 0:4, 0:COLS] = row_recv[0, 0:4, :]
    edge_send[G - 1, 4:8, 0:COLS] = row_recv[1, 0:4, :]

    def merge_columns(g, _):
        edge_send[g, :, COLS : COLS + 128] = jnp.where(
            lane % 64 < 4, col_recv[0, g], col_recv[1, g]
        )
        return 0

    lax.fori_loop(0, G, merge_columns, 0)
    edges = []
    for d in range(1, G):
        peer = jnp.bitwise_xor(gx, d)
        copy = remote(
            edge_send.at[peer, :, 0:COLS], edge_recv.at[gx],
            edge_s.at[d], edge_r.at[d], (grp, peer, gy),
        )
        copy.start()
        edges.append(copy)
    own_edge = pltpu.make_async_copy(edge_send.at[gx, :, 0:COLS], edge_recv.at[gx], local.at[7])
    own_edge.start()

    row16 = lax.broadcasted_iota(jnp.int32, (ROWS, COLS), 0)
    lane16 = lax.broadcasted_iota(jnp.int32, (ROWS, COLS), 1)
    start_x, start_y = line * ROWS, gy * COLS

    for copy in small_in:
        copy.wait()

    def mark(s, _):
        hit = jnp.logical_and(row16 == sx_ref[s] - start_x, lane16 == sy_ref[s] - start_y)
        marks[s] = jnp.where(hit, 1.0, 0.0).astype(F32)
        return 0

    lax.fori_loop(0, NSRC, mark, 0)
    ash_in.wait()

    def emit(k, _):
        for b in range(BINS):
            total = conc[b, k]
            for s in range(NSRC):
                total = total + marks[s] * rate_ref[s, b, k]
            conc[b, k] = total
        return 0

    lax.fori_loop(0, NZ, emit, 0)

    lane128 = lax.broadcasted_iota(jnp.int32, (ROWS, 128), 1)

    def pack_ash(k, sums):
        sums = list(sums)
        for b in range(BINS):
            slab = conc[b, k]
            arow_send[0, b, pl.ds(k, 1), :] = slab[ROWS - 1 : ROWS]
            arow_send[1, b, pl.ds(k, 1), :] = slab[0:1]
            at = (b % 4) * NZ + k
            spot = lane128 == at
            right = pltpu.roll(slab[:, 128:256], lax.rem(at + 1, 128), 1)
            left = pltpu.roll(slab[:, 0:128], at, 1)
            sums[b // 4] = jnp.where(spot, right, sums[b // 4])
            sums[2 + b // 4] = jnp.where(spot, left, sums[2 + b // 4])
        return tuple(sums)

    packed = lax.fori_loop(0, NZ, pack_ash, tuple(jnp.zeros((ROWS, 128), F32) for _ in range(4)))
    for side in range(2):
        for part in range(2):
            acol_send[side, part] = packed[2 * side + part]

    arows_up = remote(arow_send.at[0], arow_recv.at[0], near_s.at[4], near_r.at[4], row_up)
    arows_down = remote(arow_send.at[1], arow_recv.at[1], near_s.at[5], near_r.at[5], row_down)
    acols_up = remote(acol_send.at[0], acol_recv.at[0], near_s.at[6], near_r.at[6], (grp, gx, gy + 1))
    acols_down = remote(acol_send.at[1], acol_recv.at[1], near_s.at[7], near_r.at[7], (grp, gx, gy - 1))
    pl.when(jnp.logical_and(grp == 1, wrap_up))(lambda: pl.semaphore_wait(ready.at[1], 1))
    pl.when(line < last_line)(arows_up.start)
    pl.when(line > 0)(arows_down.start)
    pl.when(gy < GY - 1)(acols_up.start)
    pl.when(gy > 0)(acols_down.start)
    pl.when(line == 0)(lambda: clear(arow_recv.at[0]))
    pl.when(line == last_line)(lambda: clear(arow_recv.at[1]))
    pl.when(gy == 0)(lambda: clear(acol_recv.at[0]))
    pl.when(gy == GY - 1)(lambda: clear(acol_recv.at[1]))

    for copy in bulk:
        copy.wait_send()
    for copy in pairs:
        copy.start()
    for copy in bulk:
        copy.wait_recv()
    for copy in edges:
        copy.wait_recv()
    for copy in own_bulk:
        copy.wait()
    own_edge.wait()

    def pack_tile(k, sums):
        right, left = sums
        for f in range(2):
            for half in range(2):
                at = 64 * half + NZ * f + k
                rows = slice(8 * half, 8 * half + 8)
                tail = pltpu.roll(fields[f, k, rows, 128:256], lax.rem(at + 1, 128), 1)
                head = pltpu.roll(fields[f, k, rows, 0:128], at, 1)
                right = jnp.where(lane == at, tail, right)
                left = jnp.where(lane == at, head, left)
        return right, left

    right, left = lax.fori_loop(
        0, NZ, pack_tile, (jnp.zeros((8, 128), F32), jnp.zeros((8, 128), F32)), unroll=4
    )
    tcol_send[0], tcol_send[1] = right, left
    tcols_up = remote(tcol_send.at[0], tcol_recv.at[0], near_s.at[8], near_r.at[8], (grp, gx, gy + 1))
    tcols_down = remote(tcol_send.at[1], tcol_recv.at[1], near_s.at[9], near_r.at[9], (grp, gx, gy - 1))
    pl.when(gy < GY - 1)(tcols_up.start)
    pl.when(gy > 0)(tcols_down.start)
    pl.when(gy == 0)(lambda: clear(tcol_recv.at[0]))
    pl.when(gy == GY - 1)(lambda: clear(tcol_recv.at[1]))
    pl.when(gy > 0)(tcols_up.wait_recv)
    pl.when(gy < GY - 1)(tcols_down.wait_recv)

    first_row, end_row = row16 == 0, row16 == ROWS - 1
    first_lane, end_lane = lane16 == 0, lane16 == COLS - 1

    def twice(half):
        return jnp.concatenate([half, half], axis=1)

    def along_x(field, below, above):
        east = jnp.where(end_row, above, pltpu.roll(field, ROWS - 1, 0))
        west = jnp.where(first_row, below, pltpu.roll(field, 1, 0))
        return east, west

    def along_y(field, below, above):
        north = jnp.where(end_lane, twice(above), pltpu.roll(field, COLS - 1, 1))
        south = jnp.where(first_lane, twice(below), pltpu.roll(field, 1, 1))
        return north, south

    def diagnose(g, total):
        left_cols, right_cols = tcol_recv[0], tcol_recv[1]
        for lev in range(LV):
            k = LV * g + lev
            up, down = jnp.minimum(k + 1, NZ - 1), jnp.maximum(k - 1, 0)
            wind = []
            for f in range(2):
                at, lane_of = 2 * f + lev, NZ * f + k
                field = fields[f, k]
                east, west = along_x(
                    field,
                    edge_recv[g, at : at + 1, 0:COLS],
                    edge_recv[g, at + 4 : at + 5, 0:COLS],
                )
                below = jnp.concatenate(
                    [pltpu.roll(left_cols, lax.rem(128 - lane_of, 128), 1), pltpu.roll(left_cols, 64 - lane_of, 1)],
                    axis=0,
                )
                above = jnp.concatenate(
                    [pltpu.roll(right_cols, 127 - lane_of, 1), pltpu.roll(right_cols, 63 - lane_of, 1)],
                    axis=0,
                )
                north, south = along_y(field, below, above)
                slope = 0.5 * (fields[f, up] - fields[f, down])
                wind.append((field, east, west, north, south, slope))
            warm = fields[2, k]
            warm_slope = 0.5 * (fields[2, up] - fields[2, down])
            (u, ue, uw, un, us, u_slope), (v, ve, vw, vn, vs, v_slope) = wind
            xstretch, yshear = 0.5 * (ue - uw), 0.5 * (un - us)
            xshear, ystretch = 0.5 * (ve - vw), 0.5 * (vn - vs)
            total = total + (xstretch + ystretch)
            lift = jnp.clip(-lift_scale * total, -lift_limit, lift_limit)
            ret[0, k] = u + diffuse_rate * (ue + uw + un + us - 4.0 * u) - lift * u_slope
            ret[1, k] = v + diffuse_rate * (ve + vw + vn + vs - 4.0 * v) - lift * v_slope
            ret[2, k] = warm - lift * warm_slope
            if lev == 1:
                cums[g] = total
            eddy = eddy_base + eddy_slope * jnp.sqrt((xstretch - ystretch) ** 2 + (yshear + xshear) ** 2)
            mixing = mixing_base + mixing_slope * jnp.sqrt(u_slope**2 + v_slope**2) / (
                1.0 + stable_weight * jnp.maximum(warm_slope, 0.0)
            )
            height = jnp.exp(jnp.zeros((1, COLS), F32) + k.astype(F32) * (1.0 / level_decay))
            dens[k] = jnp.sqrt(warm) * height
            coef[0, k] = eddy - jnp.minimum(u, 0.0)
            coef[1, k] = eddy + jnp.maximum(u, 0.0)
            coef[2, k] = eddy - jnp.minimum(v, 0.0)
            coef[3, k] = eddy + jnp.maximum(v, 0.0)
            coef[4, k] = mixing - jnp.minimum(lift, 0.0)
            coef[5, k] = mixing + jnp.maximum(lift, 0.0)
            coef[6, k] = 1.0 - (jnp.abs(u) + jnp.abs(v) + jnp.abs(lift) + 4.0 * eddy + 2.0 * mixing)
        return total

    lax.fori_loop(0, G, diagnose, jnp.zeros((ROWS, COLS), F32))
    dens[NZ] = jnp.zeros((ROWS, COLS), F32)

    near = jnp.logical_or(own_z == 1, own_z == 2)
    near_z = jnp.where(own_z < 2, 2, 1)
    half_z = jnp.where(own_z < 2, 2, 0)
    cum_back = []
    for dx in range(4):
        peer = 4 * jnp.bitwise_xor(own_x, dx) + near_z
        copy = remote(
            cums.at[2 * (peer // 2)], cum_recv.at[own_x, own_z],
            cum_s.at[dx], cum_r.at[own_z % 2, dx], (grp, peer, gy),
        )
        copy.start()
        cum_back.append(copy)
    back = []
    for d in range(1, G):
        peer = jnp.bitwise_xor(gx, d)
        if d % 4 > 1:
            copy = remote(
                ret.at[:, LV * peer + peer % 2], met_out.at[:, peer % 2, own_x, own_z],
                ret_s.at[d], ret_r.at[d], (grp, peer, gy),
            )
        else:
            copy = remote(
                ret.at[:, pl.ds(LV * peer, LV)], met_out.at[:, :, own_x, own_z],
                ret_s.at[d], ret_r.at[d], (grp, peer, gy),
            )
        copy.start()
        back.append(copy)
    own_back = pltpu.make_async_copy(
        ret.at[:, own_levels], met_out.at[:, :, own_x, own_z], local.at[13]
    )
    own_back.start()

    pl.when(line > 0)(arows_up.wait_recv)
    pl.when(line < last_line)(arows_down.wait_recv)
    pl.when(gy > 0)(acols_up.wait_recv)
    pl.when(gy < GY - 1)(acols_down.wait_recv)

    speeds = [table_ref[class_ref[b]] for b in range(BINS)]

    def transport(k, _):
        up, down = jnp.minimum(k + 1, NZ - 1), jnp.maximum(k - 1, 0)
        for b in range(BINS):
            here = conc[b, k]
            at = (b % 4) * NZ + k
            east, west = along_x(
                here, arow_recv[0, b, pl.ds(k, 1), :], arow_recv[1, b, pl.ds(k, 1), :]
            )
            below = pltpu.roll(acol_recv[0, b // 4], lax.rem(128 - at, 128), 1)
            above = pltpu.roll(acol_recv[1, b // 4], 127 - at, 1)
            north, south = along_y(here, below, above)
            out = here * (coef[6, k] - speeds[b] * dens[k])
            out = out + conc[b, up] * (coef[4, k] + speeds[b] * dens[k + 1])
            out = out + east * coef[0, k] + west * coef[1, k]
            out = out + north * coef[2, k] + south * coef[3, k]
            ash_out[b, k] = out + conc[b, down] * coef[5, k]
        return 0

    lax.fori_loop(0, NZ, transport, 0)

    hand_on = remote(
        cum_recv.at[:, pl.ds(half_z, 2)], cum_recv.at[:, pl.ds(half_z, 2)],
        mate_s.at[0], mate_r.at[0], (grp, mate, gy),
    )

    @pl.when(near)
    def _():
        for parity in range(2):
            for dx in range(4):
                remote(
                    cums.at[0], cum_recv.at[own_x, own_z], cum_s.at[dx], cum_r.at[parity, dx], (grp, mate, gy)
                ).wait_recv()
        hand_on.start()

    pl.when(jnp.logical_not(near))(hand_on.wait_recv)
    for copy in pairs:
        copy.wait_recv()
    half = jnp.where(gx % 2 == 0, 0.5, -0.5).astype(F32)
    above_cum = (gx % 2).astype(F32)

    def step_rows(x, _):
        for j in range(2, 4):
            z = jnp.bitwise_xor(own_z, j)
            g = 4 * x + z
            edge_cols = edge_send[g, :, COLS : COLS + 128]
            wind = []
            for f in range(2):
                field = met[f, mine, x, z]
                at = 2 * f + mine
                east, west = along_x(
                    field,
                    edge_send[g, pl.ds(at, 1), 0:COLS],
                    edge_send[g, pl.ds(at + 4, 1), 0:COLS],
                )
                below = jnp.concatenate(
                    [pltpu.roll(edge_cols, 128 - at, 1), pltpu.roll(edge_cols, 64 - at, 1)], axis=0
                )
                above = jnp.concatenate(
                    [pltpu.roll(edge_cols, 123 - at, 1), pltpu.roll(edge_cols, 59 - at, 1)], axis=0
                )
                north, south = along_y(field, below, above)
                wind.append((east, west, north, south))
            (ue, uw, un, us), (ve, vw, vn, vs) = wind
            total = cum_recv[x, z] + above_cum * (0.5 * (ue - uw) + 0.5 * (vn - vs))
            lift = jnp.clip(-lift_scale * total, -lift_limit, lift_limit)
            for f in range(3):
                field = met[f, mine, x, z]
                slope = half * (partner[f, x, z] - met[f, 1 - mine, x, z])
                after = field - lift * slope
                if f < 2:
                    after = after + diffuse_rate * (sum(wind[f][1:], wind[f][0]) - 4.0 * field)
                met_out[f, mine, x, z] = after
        return 0

    lax.fori_loop(0, 4, step_rows, 0)

    for copy in pairs + edges + cum_back:
        copy.wait_send()
    pl.when(near)(hand_on.wait_send)
    own_back.wait()
    pl.when(grp < GRP - 1)(rows_up.wait_send)
    pl.when(grp > 0)(rows_down.wait_send)
    pl.when(gy < GY - 1)(cols_up.wait_send)
    pl.when(gy > 0)(cols_down.wait_send)
    pl.when(line < last_line)(arows_up.wait_send)
    pl.when(line > 0)(arows_down.wait_send)
    pl.when(gy < GY - 1)(acols_up.wait_send)
    pl.when(gy > 0)(acols_down.wait_send)
    pl.when(gy < GY - 1)(tcols_up.wait_send)
    pl.when(gy > 0)(tcols_down.wait_send)
    for copy in back:
        copy.wait_send()
    for copy in back:
        copy.wait_recv()


def write_out(ash_ref, met_ref, ash_out, met_out, done):
    copies = [pltpu.make_async_copy(ash_ref.at[b], ash_out.at[b], done.at[b]) for b in range(BINS)]
    copies += [
        pltpu.make_async_copy(met_ref.at[f], met_out.at[f], done.at[BINS + f]) for f in range(3)
    ]
    for copy in copies:
        copy.start()
    for copy in copies:
        copy.wait()


def body(wind_u, wind_v, theta, ash, src_x, src_y, src_rate, settle_class, settle_table):
    hbm = pl.BlockSpec(memory_space=pltpu.HBM)
    vmem = pl.BlockSpec(memory_space=pltpu.VMEM)
    dma = pltpu.SemaphoreType.DMA
    tiled = (LV, 4, 4, ROWS, COLS)
    ash_next, met_next = pl.pallas_call(
            kernel,
            out_shape=(
                pltpu.VMEM((BINS, NZ, ROWS, COLS), F32),
                pltpu.VMEM((3,) + tiled, F32),
            ),
            in_specs=[hbm] * 9,
            out_specs=(vmem, vmem),
            scratch_shapes=[
                pltpu.SMEM((NSRC,), jnp.int32),
                pltpu.SMEM((NSRC,), jnp.int32),
                pltpu.SMEM((NSRC, BINS, NZ), F32),
                pltpu.SMEM(settle_class.shape, jnp.int32),
                pltpu.SMEM(settle_table.shape, F32),
                pltpu.VMEM((3,) + tiled, F32),
                pltpu.VMEM((3,) + tiled[1:], F32),
                pltpu.VMEM(tiled[1:], F32),
                pltpu.VMEM((3, NZ, ROWS, COLS), F32),
                pltpu.VMEM((BINS, NZ, ROWS, COLS), F32),
                pltpu.VMEM((3, NZ, ROWS, COLS), F32),
                pltpu.VMEM((G, ROWS, COLS), F32),
                pltpu.VMEM((7, NZ, ROWS, COLS), F32),
                pltpu.VMEM((NZ + 1, ROWS, COLS), F32),
                pltpu.VMEM((NSRC, ROWS, COLS), F32),
                pltpu.VMEM((2, 8, COLS), F32),
                pltpu.VMEM((2, 8, COLS), F32),
                pltpu.VMEM((2, G, 8, 128), F32),
                pltpu.VMEM((2, G, 8, 128), F32),
                pltpu.VMEM((G, 8, COLS + 128), F32),
                pltpu.VMEM((G, 8, COLS), F32),
                pltpu.VMEM((2, BINS, NZ, COLS), F32),
                pltpu.VMEM((2, BINS, NZ, COLS), F32),
                pltpu.VMEM((2, 2, ROWS, 128), F32),
                pltpu.VMEM((2, 2, ROWS, 128), F32),
                pltpu.VMEM((2, 8, 128), F32),
                pltpu.VMEM((2, 8, 128), F32),
                dma((G,)), dma((G,)),
                dma((G,)), dma((G,)),
                dma((G,)), dma((G,)),
                dma((4,)), dma((2, 4)),
                dma((1,)), dma((1,)),
                dma((4,)), dma((4,)),
                dma((10,)), dma((10,)),
                dma((14,)),
                pltpu.SemaphoreType.REGULAR((2,)),
            ],
            compiler_params=pltpu.CompilerParams(
                collective_id=0, has_side_effects=True, vmem_limit_bytes=48 * 2**20
            ),
    )(
        *(
            pltpu.with_memory_space_constraint(array, pltpu.HBM)
            for array in (
                wind_u.reshape(tiled), wind_v.reshape(tiled), theta.reshape(tiled), ash,
                src_x, src_y, src_rate, settle_class, settle_table,
            )
        )
    )
    ash_next, met_next = pl.pallas_call(
        write_out,
        out_shape=(
            pltpu.HBM((BINS, NZ, ROWS, COLS), F32),
            pltpu.HBM((3,) + tiled, F32),
        ),
        in_specs=[vmem, vmem],
        out_specs=(hbm, hbm),
        scratch_shapes=[dma((BINS + 3,))],
        compiler_params=pltpu.CompilerParams(vmem_limit_bytes=2**20),
    )(
        pltpu.with_memory_space_constraint(ash_next, pltpu.VMEM),
        pltpu.with_memory_space_constraint(met_next, pltpu.VMEM),
    )
    return ash_next, met_next.reshape(3, LV, MROWS, COLS)


def solution(mesh):
    in_specs = (
        P("gx", "grp", "gy"),
        P("gx", "grp", "gy"),
        P("gx", "grp", "gy"),
        P(None, None, ("grp", "gx"), "gy"),
        P(),
        P(),
        P(),
        P(),
        P(),
    )
    out_specs = (P(None, None, ("grp", "gx"), "gy"), P(None, "gx", "grp", "gy"))
    return jax.shard_map(body, mesh=mesh, in_specs=in_specs, out_specs=out_specs, check_vma=False)
```

```python
import functools

import jax
import jax.numpy as jnp
from jax import lax
from jax.experimental import pallas as pl
from jax.experimental.pallas import tpu as pltpu
from jax.sharding import PartitionSpec as P

MESH = pl.DeviceIdType.MESH
F32 = jnp.float32

diffuse_rate = 0.1
lift_scale = 0.1
lift_limit = 0.15
eddy_base = 0.005
eddy_slope = 0.03
mixing_base = 0.005
mixing_slope = 0.08
stable_weight = 20.0
level_decay = 32.0

G = 16
GRP = 4
GY = 4
LV = 2
NZ = 32
ROWS = 16
COLS = 256
MROWS = 256
BINS = 8
NSRC = 16


def kernel(
    u_ref, v_ref, t_ref, ash_ref, sx_hbm, sy_hbm, rate_hbm, class_hbm, table_hbm,
    ash_out, met_out,
    sx_ref, sy_ref, rate_ref, class_ref, table_ref,
    met, partner, cum_recv, fields, conc, ret, cums, coef, dens, marks,
    row_send, row_recv, col_send, col_recv, edge_send, edge_recv,
    arow_send, arow_recv, acol_send, acol_recv, tcol_send, tcol_recv,
    bulk_s, bulk_r, edge_s, edge_r, ret_s, ret_r, cum_s, cum_r, mate_s, mate_r, part_s, part_r, near_s, near_r, local, ready,
):
    grp, gx, gy = lax.axis_index("grp"), lax.axis_index("gx"), lax.axis_index("gy")
    line = grp * G + gx
    last_line = GRP * G - 1
    wrap_up, wrap_down = gx == G - 1, gx == 0
    row_up = (grp + wrap_up.astype(jnp.int32), lax.rem(gx + 1, G), gy)
    row_down = (grp - wrap_down.astype(jnp.int32), lax.rem(gx + G - 1, G), gy)

    sources = (u_ref, v_ref, t_ref)
    met_in = [pltpu.make_async_copy(sources[f], met.at[f], local.at[f]) for f in range(3)]
    ash_in = pltpu.make_async_copy(ash_ref, conc, local.at[3])
    small_in = [
        pltpu.make_async_copy(src, dst, local.at[8 + i])
        for i, (src, dst) in enumerate(
            (
                (sx_hbm, sx_ref), (sy_hbm, sy_ref), (rate_hbm, rate_ref),
                (class_hbm, class_ref), (table_hbm, table_ref),
            )
        )
    ]

    barrier = pltpu.get_barrier_semaphore()

    def greet(device):
        pl.semaphore_signal(barrier, inc=1, device_id=device, device_id_type=MESH)

    for d in range(G - 1, 0, -1):
        greet((grp, jnp.bitwise_xor(gx, d), gy))
    pl.when(gy > 0)(lambda: greet((grp, gx, gy - 1)))
    pl.when(gy < GY - 1)(lambda: greet((grp, gx, gy + 1)))
    pl.when(jnp.logical_or(grp == 1, grp == 3))(lambda: greet((grp - 1, gx, gy)))
    pl.when(grp < GRP - 1)(lambda: greet((grp + 1, gx, gy)))
    far_down = jnp.logical_and(wrap_down, grp > 0)
    far_up = jnp.logical_and(wrap_up, grp < GRP - 1)
    pl.when(jnp.logical_and(far_down, grp != 2))(lambda: greet(row_down))
    pl.when(far_up)(lambda: greet(row_up))
    count = (
        G - 1
        + (gy > 0).astype(jnp.int32) + (gy < GY - 1).astype(jnp.int32)
        + (grp > 0).astype(jnp.int32) + (grp % 2 == 0).astype(jnp.int32)
        + far_down.astype(jnp.int32) + jnp.logical_and(far_up, grp != 1).astype(jnp.int32)
    )
    for copy in met_in:
        copy.start()
    pl.semaphore_wait(barrier, count)

    def tell(index, device):
        pl.semaphore_signal(ready.at[index], inc=1, device_id=device, device_id_type=MESH)

    pl.when(grp == 2)(lambda: tell(0, (grp - 1, gx, gy)))
    pl.when(jnp.logical_and(grp == 2, wrap_down))(lambda: tell(1, row_down))

    def remote(src, dst, send, recv, device):
        return pltpu.make_async_remote_copy(
            src_ref=src, dst_ref=dst, send_sem=send, recv_sem=recv,
            device_id=device, device_id_type=MESH,
        )

    own_levels = pl.ds(LV * gx, LV)
    own_x, own_z = gx // 4, gx % 4
    for copy in met_in:
        copy.wait()
    bulk = []
    for d in range(1, G):
        peer = jnp.bitwise_xor(gx, d)
        copy = remote(
            met.at[:, :, peer // 4, peer % 4], fields.at[:, own_levels],
            bulk_s.at[d], bulk_r.at[d], (grp, peer, gy),
        )
        copy.start()
        bulk.append(copy)
    own_bulk = [
        pltpu.make_async_copy(met.at[:, :, own_x, own_z], fields.at[:, own_levels], local.at[4])
    ]
    own_bulk[0].start()
    for copy in small_in + [ash_in]:
        copy.start()

    mine = 1 - gx % 2
    mate = jnp.bitwise_xor(gx, 1)
    pairs = []
    for j in range(2, 4):
        group = jnp.bitwise_xor(mate % 4, j)
        pairs.append(
            remote(
                met.at[:, mine, :, group], partner.at[:, :, group],
                part_s.at[j], part_r.at[j], (grp, mate, gy),
            )
        )

    lane = lax.broadcasted_iota(jnp.int32, (8, 128), 1)
    for f in range(2):
        for lev in range(LV):
            at = 2 * f + lev
            row_send[0, at : at + 1, :] = met[f, lev, 3, 3, ROWS - 1 : ROWS, :]
            row_send[1, at : at + 1, :] = met[f, lev, 0, 0, 0:1, :]
    row_send[0, 4:8, :] = jnp.zeros((4, COLS), F32)
    row_send[1, 4:8, :] = jnp.zeros((4, COLS), F32)

    def pack_columns(g, _):
        right = jnp.zeros((8, 128), F32)
        left = jnp.zeros((8, 128), F32)
        for half in range(2):
            rows = slice(8 * half, 8 * half + 8)
            for f in range(2):
                for lev in range(LV):
                    c = 64 * half + 2 * f + lev
                    tail = met[f, lev, g // 4, g % 4, rows, 128:256]
                    right = jnp.where(lane == c, pltpu.roll(tail, c + 1, 1), right)
                    head = met[f, lev, g // 4, g % 4, rows, 0:128]
                    left = jnp.where(lane == c + 4, pltpu.roll(head, c + 4, 1), left)
        col_send[0, g] = right
        col_send[1, g] = left
        return 0

    lax.fori_loop(0, G, pack_columns, 0)

    rows_up = remote(row_send.at[0], row_recv.at[0], near_s.at[0], near_r.at[0], (grp + 1, gx, gy))
    rows_down = remote(row_send.at[1], row_recv.at[1], near_s.at[1], near_r.at[1], (grp - 1, gx, gy))
    cols_up = remote(col_send.at[0], col_recv.at[0], near_s.at[2], near_r.at[2], (grp, gx, gy + 1))
    cols_down = remote(col_send.at[1], col_recv.at[1], near_s.at[3], near_r.at[3], (grp, gx, gy - 1))

    def clear(ref):
        ref[...] = jnp.zeros(ref.shape, F32)

    pl.when(gy < GY - 1)(cols_up.start)
    pl.when(gy > 0)(cols_down.start)
    pl.when(jnp.logical_and(grp < GRP - 1, grp != 1))(rows_up.start)
    pl.when(grp > 0)(rows_down.start)
    pl.when(grp == 0)(lambda: clear(row_recv.at[0]))
    pl.when(grp == GRP - 1)(lambda: clear(row_recv.at[1]))
    pl.when(gy == 0)(lambda: clear(col_recv.at[0]))
    pl.when(gy == GY - 1)(lambda: clear(col_recv.at[1]))

    def pack_rows(g, _):
        before, after = jnp.maximum(g - 1, 0), jnp.minimum(g + 1, G - 1)
        for f in range(2):
            for lev in range(LV):
                at = 2 * f + lev
                edge_send[g, at : at + 1, 0:COLS] = met[f, lev, before // 4, before % 4, ROWS - 1 : ROWS, :]
                edge_send[g, at + 4 : at + 5, 0:COLS] = met[f, lev, after // 4, after % 4, 0:1, :]
        return 0

    lax.fori_loop(0, G, pack_rows, 0)

    @pl.when(grp == 1)
    def _():
        pl.semaphore_wait(ready.at[0], 1)
        rows_up.start()

    pl.when(grp > 0)(rows_up.wait_recv)
    pl.when(grp < GRP - 1)(rows_down.wait_recv)
    pl.when(gy > 0)(cols_up.wait_recv)
    pl.when(gy < GY - 1)(cols_down.wait_recv)
    edge_send[0, 0:4, 0:COLS] = row_recv[0, 0:4, :]
    edge_send[G - 1, 4:8, 0:COLS] = row_recv[1, 0:4, :]

    def merge_columns(g, _):
        edge_send[g, :, COLS : COLS + 128] = jnp.where(
            lane % 64 < 4, col_recv[0, g], col_recv[1, g]
        )
        return 0

    lax.fori_loop(0, G, merge_columns, 0)
    edges = []
    for d in range(1, G):
        peer = jnp.bitwise_xor(gx, d)
        copy = remote(
            edge_send.at[peer, :, 0:COLS], edge_recv.at[gx],
            edge_s.at[d], edge_r.at[d], (grp, peer, gy),
        )
        copy.start()
        edges.append(copy)
    own_edge = pltpu.make_async_copy(edge_send.at[gx, :, 0:COLS], edge_recv.at[gx], local.at[7])
    own_edge.start()

    row16 = lax.broadcasted_iota(jnp.int32, (ROWS, COLS), 0)
    lane16 = lax.broadcasted_iota(jnp.int32, (ROWS, COLS), 1)
    start_x, start_y = line * ROWS, gy * COLS

    for copy in small_in:
        copy.wait()

    def mark(s, _):
        hit = jnp.logical_and(row16 == sx_ref[s] - start_x, lane16 == sy_ref[s] - start_y)
        marks[s] = jnp.where(hit, 1.0, 0.0).astype(F32)
        return 0

    lax.fori_loop(0, NSRC, mark, 0)
    ash_in.wait()

    def emit(k, _):
        for b in range(BINS):
            total = conc[b, k]
            for s in range(NSRC):
                total = total + marks[s] * rate_ref[s, b, k]
            conc[b, k] = total
        return 0

    lax.fori_loop(0, NZ, emit, 0)

    lane128 = lax.broadcasted_iota(jnp.int32, (ROWS, 128), 1)

    def pack_ash(k, sums):
        sums = list(sums)
        for b in range(BINS):
            slab = conc[b, k]
            arow_send[0, b, pl.ds(k, 1), :] = slab[ROWS - 1 : ROWS]
            arow_send[1, b, pl.ds(k, 1), :] = slab[0:1]
            at = (b % 4) * NZ + k
            spot = lane128 == at
            right = pltpu.roll(slab[:, 128:256], lax.rem(at + 1, 128), 1)
            left = pltpu.roll(slab[:, 0:128], at, 1)
            sums[b // 4] = jnp.where(spot, right, sums[b // 4])
            sums[2 + b // 4] = jnp.where(spot, left, sums[2 + b // 4])
        return tuple(sums)

    packed = lax.fori_loop(0, NZ, pack_ash, tuple(jnp.zeros((ROWS, 128), F32) for _ in range(4)))
    for side in range(2):
        for part in range(2):
            acol_send[side, part] = packed[2 * side + part]

    arows_up = remote(arow_send.at[0], arow_recv.at[0], near_s.at[4], near_r.at[4], row_up)
    arows_down = remote(arow_send.at[1], arow_recv.at[1], near_s.at[5], near_r.at[5], row_down)
    acols_up = remote(acol_send.at[0], acol_recv.at[0], near_s.at[6], near_r.at[6], (grp, gx, gy + 1))
    acols_down = remote(acol_send.at[1], acol_recv.at[1], near_s.at[7], near_r.at[7], (grp, gx, gy - 1))
    pl.when(jnp.logical_and(grp == 1, wrap_up))(lambda: pl.semaphore_wait(ready.at[1], 1))
    pl.when(line < last_line)(arows_up.start)
    pl.when(line > 0)(arows_down.start)
    pl.when(gy < GY - 1)(acols_up.start)
    pl.when(gy > 0)(acols_down.start)
    pl.when(line == 0)(lambda: clear(arow_recv.at[0]))
    pl.when(line == last_line)(lambda: clear(arow_recv.at[1]))
    pl.when(gy == 0)(lambda: clear(acol_recv.at[0]))
    pl.when(gy == GY - 1)(lambda: clear(acol_recv.at[1]))

    for copy in bulk:
        copy.wait_send()
    for copy in pairs:
        copy.start()
    for copy in bulk:
        copy.wait_recv()
    for copy in edges:
        copy.wait_recv()
    for copy in own_bulk:
        copy.wait()
    own_edge.wait()

    def pack_tile(k, sums):
        right, left = sums
        for f in range(2):
            for half in range(2):
                at = 64 * half + NZ * f + k
                rows = slice(8 * half, 8 * half + 8)
                tail = pltpu.roll(fields[f, k, rows, 128:256], lax.rem(at + 1, 128), 1)
                head = pltpu.roll(fields[f, k, rows, 0:128], at, 1)
                right = jnp.where(lane == at, tail, right)
                left = jnp.where(lane == at, head, left)
        return right, left

    right, left = lax.fori_loop(
        0, NZ, pack_tile, (jnp.zeros((8, 128), F32), jnp.zeros((8, 128), F32)), unroll=4
    )
    tcol_send[0], tcol_send[1] = right, left
    tcols_up = remote(tcol_send.at[0], tcol_recv.at[0], near_s.at[8], near_r.at[8], (grp, gx, gy + 1))
    tcols_down = remote(tcol_send.at[1], tcol_recv.at[1], near_s.at[9], near_r.at[9], (grp, gx, gy - 1))
    pl.when(gy < GY - 1)(tcols_up.start)
    pl.when(gy > 0)(tcols_down.start)
    pl.when(gy == 0)(lambda: clear(tcol_recv.at[0]))
    pl.when(gy == GY - 1)(lambda: clear(tcol_recv.at[1]))
    pl.when(gy > 0)(tcols_up.wait_recv)
    pl.when(gy < GY - 1)(tcols_down.wait_recv)

    first_row, end_row = row16 == 0, row16 == ROWS - 1
    first_lane, end_lane = lane16 == 0, lane16 == COLS - 1

    def twice(half):
        return jnp.concatenate([half, half], axis=1)

    def along_x(field, below, above):
        east = jnp.where(end_row, above, pltpu.roll(field, ROWS - 1, 0))
        west = jnp.where(first_row, below, pltpu.roll(field, 1, 0))
        return east, west

    def along_y(field, below, above):
        north = jnp.where(end_lane, twice(above), pltpu.roll(field, COLS - 1, 1))
        south = jnp.where(first_lane, twice(below), pltpu.roll(field, 1, 1))
        return north, south

    def diagnose(g, total):
        left_cols, right_cols = tcol_recv[0], tcol_recv[1]
        for lev in range(LV):
            k = LV * g + lev
            up, down = jnp.minimum(k + 1, NZ - 1), jnp.maximum(k - 1, 0)
            wind = []
            for f in range(2):
                at, lane_of = 2 * f + lev, NZ * f + k
                field = fields[f, k]
                east, west = along_x(
                    field,
                    edge_recv[g, at : at + 1, 0:COLS],
                    edge_recv[g, at + 4 : at + 5, 0:COLS],
                )
                below = jnp.concatenate(
                    [pltpu.roll(left_cols, lax.rem(128 - lane_of, 128), 1), pltpu.roll(left_cols, 64 - lane_of, 1)],
                    axis=0,
                )
                above = jnp.concatenate(
                    [pltpu.roll(right_cols, 127 - lane_of, 1), pltpu.roll(right_cols, 63 - lane_of, 1)],
                    axis=0,
                )
                north, south = along_y(field, below, above)
                slope = 0.5 * (fields[f, up] - fields[f, down])
                wind.append((field, east, west, north, south, slope))
            warm = fields[2, k]
            warm_slope = 0.5 * (fields[2, up] - fields[2, down])
            (u, ue, uw, un, us, u_slope), (v, ve, vw, vn, vs, v_slope) = wind
            xstretch, yshear = 0.5 * (ue - uw), 0.5 * (un - us)
            xshear, ystretch = 0.5 * (ve - vw), 0.5 * (vn - vs)
            total = total + (xstretch + ystretch)
            lift = jnp.clip(-lift_scale * total, -lift_limit, lift_limit)
            ret[0, k] = u + diffuse_rate * (ue + uw + un + us - 4.0 * u) - lift * u_slope
            ret[1, k] = v + diffuse_rate * (ve + vw + vn + vs - 4.0 * v) - lift * v_slope
            ret[2, k] = warm - lift * warm_slope
            if lev == 1:
                cums[g] = total
            eddy = eddy_base + eddy_slope * jnp.sqrt((xstretch - ystretch) ** 2 + (yshear + xshear) ** 2)
            mixing = mixing_base + mixing_slope * jnp.sqrt(u_slope**2 + v_slope**2) / (
                1.0 + stable_weight * jnp.maximum(warm_slope, 0.0)
            )
            height = jnp.exp(jnp.zeros((1, COLS), F32) + k.astype(F32) * (1.0 / level_decay))
            dens[k] = jnp.sqrt(warm) * height
            coef[0, k] = eddy - jnp.minimum(u, 0.0)
            coef[1, k] = eddy + jnp.maximum(u, 0.0)
            coef[2, k] = eddy - jnp.minimum(v, 0.0)
            coef[3, k] = eddy + jnp.maximum(v, 0.0)
            coef[4, k] = mixing - jnp.minimum(lift, 0.0)
            coef[5, k] = mixing + jnp.maximum(lift, 0.0)
            coef[6, k] = 1.0 - (jnp.abs(u) + jnp.abs(v) + jnp.abs(lift) + 4.0 * eddy + 2.0 * mixing)
        return total

    lax.fori_loop(0, G, diagnose, jnp.zeros((ROWS, COLS), F32))
    dens[NZ] = jnp.zeros((ROWS, COLS), F32)

    near = jnp.logical_or(own_z == 1, own_z == 2)
    near_z = jnp.where(own_z < 2, 2, 1)
    half_z = jnp.where(own_z < 2, 2, 0)
    cum_back = []
    for dx in range(4):
        peer = 4 * jnp.bitwise_xor(own_x, dx) + near_z
        copy = remote(
            cums.at[2 * (peer // 2)], cum_recv.at[own_x, own_z],
            cum_s.at[dx], cum_r.at[own_z % 2, dx], (grp, peer, gy),
        )
        copy.start()
        cum_back.append(copy)
    back = []
    for d in range(1, G):
        peer = jnp.bitwise_xor(gx, d)
        if d % 4 > 1:
            copy = remote(
                ret.at[:, LV * peer + peer % 2], met_out.at[:, peer % 2, own_x, own_z],
                ret_s.at[d], ret_r.at[d], (grp, peer, gy),
            )
        else:
            copy = remote(
                ret.at[:, pl.ds(LV * peer, LV)], met_out.at[:, :, own_x, own_z],
                ret_s.at[d], ret_r.at[d], (grp, peer, gy),
            )
        copy.start()
        back.append(copy)
    own_back = pltpu.make_async_copy(
        ret.at[:, own_levels], met_out.at[:, :, own_x, own_z], local.at[13]
    )
    own_back.start()

    pl.when(line > 0)(arows_up.wait_recv)
    pl.when(line < last_line)(arows_down.wait_recv)
    pl.when(gy > 0)(acols_up.wait_recv)
    pl.when(gy < GY - 1)(acols_down.wait_recv)

    speeds = [table_ref[class_ref[b]] for b in range(BINS)]

    def transport(k, _):
        up, down = jnp.minimum(k + 1, NZ - 1), jnp.maximum(k - 1, 0)
        for b in range(BINS):
            here = conc[b, k]
            at = (b % 4) * NZ + k
            east, west = along_x(
                here, arow_recv[0, b, pl.ds(k, 1), :], arow_recv[1, b, pl.ds(k, 1), :]
            )
            below = pltpu.roll(acol_recv[0, b // 4], lax.rem(128 - at, 128), 1)
            above = pltpu.roll(acol_recv[1, b // 4], 127 - at, 1)
            north, south = along_y(here, below, above)
            out = here * (coef[6, k] - speeds[b] * dens[k])
            out = out + conc[b, up] * (coef[4, k] + speeds[b] * dens[k + 1])
            out = out + east * coef[0, k] + west * coef[1, k]
            out = out + north * coef[2, k] + south * coef[3, k]
            ash_out[b, k] = out + conc[b, down] * coef[5, k]
        return 0

    lax.fori_loop(0, NZ, transport, 0)

    hand_on = remote(
        cum_recv.at[:, pl.ds(half_z, 2)], cum_recv.at[:, pl.ds(half_z, 2)],
        mate_s.at[0], mate_r.at[0], (grp, mate, gy),
    )

    @pl.when(near)
    def _():
        for parity in range(2):
            for dx in range(4):
                remote(
                    cums.at[0], cum_recv.at[own_x, own_z], cum_s.at[dx], cum_r.at[parity, dx], (grp, mate, gy)
                ).wait_recv()
        hand_on.start()

    pl.when(jnp.logical_not(near))(hand_on.wait_recv)
    for copy in pairs:
        copy.wait_recv()
    half = jnp.where(gx % 2 == 0, 0.5, -0.5).astype(F32)
    above_cum = (gx % 2).astype(F32)

    def step_rows(x, _):
        for j in range(2, 4):
            z = jnp.bitwise_xor(own_z, j)
            g = 4 * x + z
            edge_cols = edge_send[g, :, COLS : COLS + 128]
            wind = []
            for f in range(2):
                field = met[f, mine, x, z]
                at = 2 * f + mine
                east, west = along_x(
                    field,
                    edge_send[g, pl.ds(at, 1), 0:COLS],
                    edge_send[g, pl.ds(at + 4, 1), 0:COLS],
                )
                below = jnp.concatenate(
                    [pltpu.roll(edge_cols, lax.rem(128 - at, 128), 1), pltpu.roll(edge_cols, 64 - at, 1)], axis=0
                )
                above = jnp.concatenate(
                    [pltpu.roll(edge_cols, 123 - at, 1), pltpu.roll(edge_cols, 59 - at, 1)], axis=0
                )
                north, south = along_y(field, below, above)
                wind.append((east, west, north, south))
            (ue, uw, un, us), (ve, vw, vn, vs) = wind
            total = cum_recv[x, z] + above_cum * (0.5 * (ue - uw) + 0.5 * (vn - vs))
            lift = jnp.clip(-lift_scale * total, -lift_limit, lift_limit)
            for f in range(3):
                field = met[f, mine, x, z]
                slope = half * (partner[f, x, z] - met[f, 1 - mine, x, z])
                after = field - lift * slope
                if f < 2:
                    after = after + diffuse_rate * (sum(wind[f][1:], wind[f][0]) - 4.0 * field)
                met_out[f, mine, x, z] = after
        return 0

    lax.fori_loop(0, 4, step_rows, 0)

    for copy in pairs + edges + cum_back:
        copy.wait_send()
    pl.when(near)(hand_on.wait_send)
    own_back.wait()
    pl.when(grp < GRP - 1)(rows_up.wait_send)
    pl.when(grp > 0)(rows_down.wait_send)
    pl.when(gy < GY - 1)(cols_up.wait_send)
    pl.when(gy > 0)(cols_down.wait_send)
    pl.when(line < last_line)(arows_up.wait_send)
    pl.when(line > 0)(arows_down.wait_send)
    pl.when(gy < GY - 1)(acols_up.wait_send)
    pl.when(gy > 0)(acols_down.wait_send)
    pl.when(gy < GY - 1)(tcols_up.wait_send)
    pl.when(gy > 0)(tcols_down.wait_send)
    for copy in back:
        copy.wait_send()
    for copy in back:
        copy.wait_recv()


def write_out(ash_ref, met_ref, ash_out, met_out, done):
    copies = [pltpu.make_async_copy(ash_ref.at[b], ash_out.at[b], done.at[b]) for b in range(BINS)]
    copies += [
        pltpu.make_async_copy(met_ref.at[f], met_out.at[f], done.at[BINS + f]) for f in range(3)
    ]
    for copy in copies:
        copy.start()
    for copy in copies:
        copy.wait()


def body(wind_u, wind_v, theta, ash, src_x, src_y, src_rate, settle_class, settle_table):
    hbm = pl.BlockSpec(memory_space=pltpu.HBM)
    vmem = pl.BlockSpec(memory_space=pltpu.VMEM)
    dma = pltpu.SemaphoreType.DMA
    tiled = (LV, 4, 4, ROWS, COLS)
    ash_next, met_next = pl.pallas_call(
            kernel,
            out_shape=(
                pltpu.VMEM((BINS, NZ, ROWS, COLS), F32),
                pltpu.VMEM((3,) + tiled, F32),
            ),
            in_specs=[hbm] * 9,
            out_specs=(vmem, vmem),
            scratch_shapes=[
                pltpu.SMEM((NSRC,), jnp.int32),
                pltpu.SMEM((NSRC,), jnp.int32),
                pltpu.SMEM((NSRC, BINS, NZ), F32),
                pltpu.SMEM(settle_class.shape, jnp.int32),
                pltpu.SMEM(settle_table.shape, F32),
                pltpu.VMEM((3,) + tiled, F32),
                pltpu.VMEM((3,) + tiled[1:], F32),
                pltpu.VMEM(tiled[1:], F32),
                pltpu.VMEM((3, NZ, ROWS, COLS), F32),
                pltpu.VMEM((BINS, NZ, ROWS, COLS), F32),
                pltpu.VMEM((3, NZ, ROWS, COLS), F32),
                pltpu.VMEM((G, ROWS, COLS), F32),
                pltpu.VMEM((7, NZ, ROWS, COLS), F32),
                pltpu.VMEM((NZ + 1, ROWS, COLS), F32),
                pltpu.VMEM((NSRC, ROWS, COLS), F32),
                pltpu.VMEM((2, 8, COLS), F32),
                pltpu.VMEM((2, 8, COLS), F32),
                pltpu.VMEM((2, G, 8, 128), F32),
                pltpu.VMEM((2, G, 8, 128), F32),
                pltpu.VMEM((G, 8, COLS + 128), F32),
                pltpu.VMEM((G, 8, COLS), F32),
                pltpu.VMEM((2, BINS, NZ, COLS), F32),
                pltpu.VMEM((2, BINS, NZ, COLS), F32),
                pltpu.VMEM((2, 2, ROWS, 128), F32),
                pltpu.VMEM((2, 2, ROWS, 128), F32),
                pltpu.VMEM((2, 8, 128), F32),
                pltpu.VMEM((2, 8, 128), F32),
                dma((G,)), dma((G,)),
                dma((G,)), dma((G,)),
                dma((G,)), dma((G,)),
                dma((4,)), dma((2, 4)),
                dma((1,)), dma((1,)),
                dma((4,)), dma((4,)),
                dma((10,)), dma((10,)),
                dma((14,)),
                pltpu.SemaphoreType.REGULAR((2,)),
            ],
            compiler_params=pltpu.CompilerParams(
                collective_id=0, has_side_effects=True, vmem_limit_bytes=32 * 2**20
            ),
    )(
        *(
            pltpu.with_memory_space_constraint(array, pltpu.HBM)
            for array in (
                wind_u.reshape(tiled), wind_v.reshape(tiled), theta.reshape(tiled), ash,
                src_x, src_y, src_rate, settle_class, settle_table,
            )
        )
    )
    ash_next, met_next = pl.pallas_call(
        write_out,
        out_shape=(
            pltpu.HBM((BINS, NZ, ROWS, COLS), F32),
            pltpu.HBM((3,) + tiled, F32),
        ),
        in_specs=[vmem, vmem],
        out_specs=(hbm, hbm),
        scratch_shapes=[dma((BINS + 3,))],
        compiler_params=pltpu.CompilerParams(vmem_limit_bytes=2**20),
    )(
        pltpu.with_memory_space_constraint(ash_next, pltpu.VMEM),
        pltpu.with_memory_space_constraint(met_next, pltpu.VMEM),
    )
    return ash_next, met_next.reshape(3, LV, MROWS, COLS)


def solution(mesh):
    in_specs = (
        P("gx", "grp", "gy"),
        P("gx", "grp", "gy"),
        P("gx", "grp", "gy"),
        P(None, None, ("grp", "gx"), "gy"),
        P(),
        P(),
        P(),
        P(),
        P(),
    )
    out_specs = (P(None, None, ("grp", "gx"), "gy"), P(None, "gx", "grp", "gy"))
    return jax.shard_map(body, mesh=mesh, in_specs=in_specs, out_specs=out_specs, check_vma=False)
```
